256 devices in a mesh: frame: 32 (over z, x), head: 8 (over y, core).
Axes of the slice: x: 4, y: 4, z: 8, core: 2. Of those that a mesh axis runs over, the one named last changes fastest.
Arguments:
- qkv: bfloat16 [32768, 3, 3072], P('frame', None, 'head'), may hold values from -24 to 24
- head_kinds: int32 [24], replicated, may hold values from 0 to 1
- out_weight: bfloat16 [3072, 3072], P('head'), may hold values from -0.375 to 0.375
Outputs:
- projected: bfloat16 [32768, 3072], P('frame', 'head')
The draws below stay inside these ranges and needn't reach their ends.
All inputs are finite; a program needn't handle non-finite values.
Results may differ from the reference program's by a relative error of at most 0.017.
Values may be sent and summed in bfloat16 or wider, within the bound.
A program may use at most 64 MiB of HBM per device.

```python
import jax
import jax.numpy as jnp
from jax import lax

HEADS = 24
HD = 128
TOK_F = 1024
FRAMES = 32
TOKENS = 32768
DIM = 3072
N_HEAD = 8


def draw_qkv(key, part):
    key = jax.random.fold_in(key, 17)
    key_base = jax.random.fold_in(key, 0)
    factors = jnp.array([1.6, 1.0, 1.0], jnp.float32).reshape(1, 3, 1)
    base = jax.random.normal(key_base, (TOKENS, 3, DIM), jnp.float32) * factors
    return base.astype(jnp.bfloat16)


def set_ends(values, rng, least, largest):
    dims = values.shape
    index_at = [jax.random.randint(jax.random.fold_in(rng, axis), (), 0, dims[axis]) for axis in range(len(dims))]
    values = values.at[tuple(index_at)].set(least)
    longest = dims.index(max(dims))
    index_at[longest] = (index_at[longest] + 1) % dims[longest]
    return values.at[tuple(index_at)].set(largest)


def steps_of(own_key, dims, pieces, least, largest):
    def one(axis_at, parts):
        draws = jax.random.uniform(jax.random.fold_in(jax.random.fold_in(own_key, 6), axis_at), (parts,), jnp.float32, least / len(pieces), largest / len(pieces))
        return jnp.repeat(jnp.exp(draws), dims[axis_at] // parts).reshape((-1,) + (1,) * (len(dims) - axis_at - 1))

    gain = one(*pieces[0])
    for cut in pieces[1:]:
        gain = gain * one(*cut)
    return gain


def scatter_about(own_key, extent, deviation, most, shards=(), kind=jnp.bfloat16):
    values = jax.random.normal(own_key, extent, jnp.float32) * deviation
    if len(shards) > 0:
        values = steps_of(own_key, extent, shards, -0.22, 0.18) * values
    return jnp.clip(values, min=-most, max=most).astype(kind)


def setup_inputs(seed: int = 0) -> dict:
    key_of = jax.random.split(jax.random.key(seed), 4)
    return {
        "qkv": draw_qkv(jax.random.fold_in(key_of[3], 71), 0),
        "head_kinds": set_ends(jax.random.randint(key_of[1], (HEADS,), 0, 2), jax.random.fold_in(key_of[1], 1), 0, 1).astype(jnp.int32),
        "out_weight": scatter_about(key_of[2], (DIM, DIM), (2 * HD) ** -0.5, 0.375, ((0, 8),)),
    }


def attend(queries, key_rows, value_rows, usable):
    scores = jnp.dot(queries, key_rows.T, preferred_element_type=jnp.float32) * (HD ** -0.5)
    scores = jnp.where(usable, scores, -1e30)
    row_max = jnp.max(scores, axis=-1, keepdims=True)
    expo = jnp.exp(scores - row_max)
    normalizer = jnp.sum(expo, axis=-1, keepdims=True)
    weights = expo.astype(jnp.bfloat16)
    return (jnp.dot(weights, value_rows, preferred_element_type=jnp.float32) / normalizer).astype(jnp.bfloat16)


def reference(qkv, head_kinds, out_weight):
    queries = qkv[:, 0, :].reshape(FRAMES, TOK_F, HEADS, HD)
    key_all = qkv[:, 1, :].reshape(FRAMES, TOK_F, HEADS, HD)
    value_all = qkv[:, 2, :].reshape(FRAMES, TOK_F, HEADS, HD)

    def spatial(head):
        qh = queries[:, :, head]
        kh = key_all[:, :, head]
        vh = value_all[:, :, head]

        def one_frame(frame):
            key_rows = jnp.concatenate([kh[frame], kh[0]], axis=0)
            value_rows = jnp.concatenate([vh[frame], vh[0]], axis=0)
            column = jnp.arange(2 * TOK_F, dtype=jnp.int32)
            usable = (column < TOK_F) | (frame != 0)
            return attend(qh[frame], key_rows, value_rows, usable[None, :])

        return lax.map(one_frame, jnp.arange(FRAMES, dtype=jnp.int32))

    def temporal(head):
        qh = queries[:, :, head].astype(jnp.float32)
        kh = key_all[:, :, head].astype(jnp.float32)
        vh = value_all[:, :, head].astype(jnp.float32)
        scores = jnp.einsum('fpd,gpd->pfg', qh, kh) * (HD ** -0.5)
        row_max = jnp.max(scores, axis=-1, keepdims=True)
        expo = jnp.exp(scores - row_max)
        normalizer = jnp.sum(expo, axis=-1)
        weights = expo.astype(jnp.bfloat16).astype(jnp.float32)
        mixed = jnp.einsum('pfg,gpd->fpd', weights, vh)
        return (mixed / normalizer.T[:, :, None]).astype(jnp.bfloat16)

    def per_head(head):
        return lax.cond(head_kinds[head] == 1, temporal, spatial, head)

    outputs = lax.map(per_head, jnp.arange(HEADS, dtype=jnp.int32))
    attended = outputs.transpose(1, 2, 0, 3).reshape(TOKENS, DIM)
    group_width = DIM // N_HEAD
    running = jnp.zeros((TOKENS, DIM), jnp.float32)
    for group in range(N_HEAD):
        lower = group * group_width
        partial_term = jnp.dot(attended[:, lower:lower + group_width], out_weight[lower:lower + group_width],
                               preferred_element_type=jnp.float32).astype(jnp.bfloat16)
        partial_term = lax.optimization_barrier(partial_term)
        running = running + partial_term.astype(jnp.float32)
    return running.astype(jnp.bfloat16)
```

```python
import functools

import jax
import jax.numpy as jnp
from jax import lax
from jax.experimental import pallas as pl
from jax.experimental.pallas import tpu as pltpu
from jax.sharding import PartitionSpec as P

HD = 128
MESH = pl.DeviceIdType.MESH
NX = 4
NZ = 8
NF = NX * NZ
NY = 4
HL = 3
HC = 2 * HL
TOK = 1024
HALF = TOK // 2
ROWS = HALF // NF
CH = TOK // NF
WL = HL * HD
WC = HC * HD
QB = 256
SCALE = HD ** -0.5


def rdma(src, dst, send_sem, recv_sem, where):
    return pltpu.make_async_remote_copy(
        src_ref=src, dst_ref=dst, send_sem=send_sem, recv_sem=recv_sem,
        device_id=where, device_id_type=MESH,
    )


def dot_t(a, b):
    return lax.dot_general(a, b, (((1,), (1,)), ((), ())), preferred_element_type=jnp.float32)


def dot(a, b):
    return jnp.dot(a, b, preferred_element_type=jnp.float32)


def kernel(
    slots, kinds, qkv, weight, out,
    qkv6, stage, recv, ostage, oret, kv0, satt, att6, att, wfull,
    far_out, far_in, near_out, near_in, swap_out,
    loc_sem, px_send, px_recv, a_send, a_recv, o_send, o_recv,
    sc_send, sc_recv, z_send, z_recv, x_send, x_recv, y_send, y_recv,
):
    me = lax.axis_index("frame")
    mh = lax.axis_index("head")
    z, x = me // NX, me % NX
    y, c = mh // 2, mh % 2
    other = 1 - c
    partner = {"head": y * 2 + other}
    plus = {"head": lax.rem(y + 1, NY) * 2 + c}
    minus = {"head": lax.rem(y + NY - 1, NY) * 2 + c}

    barrier = pltpu.get_barrier_semaphore()

    def greet(j, carry):
        pl.semaphore_signal(
            barrier, inc=1, device_id={"frame": lax.rem(me + j, NF)}, device_id_type=MESH
        )
        return carry

    lax.fori_loop(1, NF, greet, 0)
    for who in (partner, plus, minus):
        pl.semaphore_signal(barrier, inc=1, device_id=who, device_id_type=MESH)

    my_rows = pl.ds(pl.multiple_of(c * HALF, HALF), HALF)
    other_rows = pl.ds(pl.multiple_of(other * HALF, HALF), HALF)
    my_lanes = pl.ds(pl.multiple_of(c * WL, HD), WL)
    other_lanes = pl.ds(pl.multiple_of(other * WL, HD), WL)
    my_wrows = pl.ds(pl.multiple_of(c * WL, HD), WL)

    own_qkv = pltpu.make_async_copy(qkv.at[:, my_rows, :], qkv6.at[:, :, my_lanes], loc_sem.at[0])
    own_qkv.start()
    own_w = pltpu.make_async_copy(weight, wfull.at[my_wrows, :], loc_sem.at[1])
    own_w.start()

    pl.semaphore_wait(barrier, NF - 1 + 3)

    swap = rdma(
        qkv.at[:, other_rows, :], qkv6.at[:, :, my_lanes], px_send.at[0], px_recv.at[0], partner
    )
    swap.start()

    @pl.when(me == 0)
    def _():
        own_chunk = pltpu.make_async_copy(
            qkv.at[pl.ds(1, 2), pl.ds(0, CH), :], kv0.at[:, 0, 0], sc_recv
        )
        own_chunk.start()

        def scatter(j, carry):
            rows = pl.ds(pl.multiple_of(j * CH, CH), CH)
            rdma(
                qkv.at[pl.ds(1, 2), rows, :], kv0.at[:, j // NX, j % NX],
                sc_send.at[j], sc_recv, {"frame": j},
            ).start()
            return carry

        lax.fori_loop(1, NF, scatter, 0)

    swap_w = rdma(weight, wfull.at[my_wrows, :], px_send.at[1], px_recv.at[1], partner)
    swap_w.start()

    own_qkv.wait()
    rdma(
        qkv.at[:, my_rows, :], qkv6.at[:, :, other_lanes], px_send.at[0], px_recv.at[0], partner
    ).wait_recv()

    for t in range(slots):
        for i in range(3):
            stage[:, t, i] = qkv6[i, :, t * HD : (t + 1) * HD].reshape(NF, ROWS, HD)

    def send_parts(j, carry):
        to = lax.rem(me + j, NF)
        rdma(stage.at[to], recv.at[me], a_send.at[to], a_recv.at[me], {"frame": to}).start()
        return carry

    lax.fori_loop(1, NF, send_parts, 0)
    recv[pl.ds(me, 1)] = stage[pl.ds(me, 1)]

    pltpu.make_async_copy(
        qkv.at[pl.ds(1, 2), pl.ds(0, CH), :], kv0.at[:, z, x], sc_recv
    ).wait()

    def send_z(j, carry):
        to = lax.rem(z + j, NZ)
        rdma(
            kv0.at[:, z, x], kv0.at[:, z, x], z_send.at[to], z_recv.at[z], {"frame": to * NX + x}
        ).start()
        return carry

    lax.fori_loop(1, NZ, send_z, 0)

    def wait_z(j, carry):
        at = lax.rem(z + j, NZ)
        rdma(
            kv0.at[:, at, x], kv0.at[:, at, x], z_send.at[at], z_recv.at[at],
            {"frame": at * NX + x},
        ).wait_recv()
        return carry

    lax.fori_loop(1, NZ, wait_z, 0)

    def send_x(j, carry):
        to = lax.rem(x + j, NX)
        rdma(
            kv0.at[:, :, x], kv0.at[:, :, x], x_send.at[to], x_recv.at[x], {"frame": z * NX + to}
        ).start()
        return carry

    lax.fori_loop(1, NX, send_x, 0)

    def wait_x(j, carry):
        at = lax.rem(x + j, NX)
        rdma(
            kv0.at[:, :, at], kv0.at[:, :, at], x_send.at[at], x_recv.at[at],
            {"frame": z * NX + at},
        ).wait_recv()
        return carry

    lax.fori_loop(1, NX, wait_x, 0)

    for h in range(HL):
        lanes = slice(h * HD, (h + 1) * HD)

        def spatial(b, carry, lanes=lanes):
            rows = pl.ds(pl.multiple_of(b * QB, QB), QB)
            q = qkv[0, rows, lanes]
            s_own = dot_t(q, qkv[1, :, lanes]) * SCALE
            s_first = dot_t(q, kv0[0, :, :, :, lanes].reshape(TOK, HD)) * SCALE
            s_first = jnp.where(me == 0, -1e30, s_first)
            top = jnp.maximum(
                jnp.max(s_own, axis=-1, keepdims=True), jnp.max(s_first, axis=-1, keepdims=True)
            )
            e_own = jnp.exp(s_own - top)
            e_first = jnp.exp(s_first - top)
            norm = jnp.sum(e_own, axis=-1, keepdims=True) + jnp.sum(e_first, axis=-1, keepdims=True)
            mixed = dot(e_own.astype(jnp.bfloat16), qkv[2, :, lanes])
            mixed += dot(
                e_first.astype(jnp.bfloat16), kv0[1, :, :, :, lanes].reshape(TOK, HD)
            )
            satt[rows, lanes] = (mixed / norm).astype(jnp.bfloat16)
            return carry

        lax.fori_loop(0, TOK // QB, spatial, 0)

    swap_s = rdma(
        satt.at[other_rows, :], att6.at[:, my_lanes], px_send.at[2], px_recv.at[2], partner
    )
    swap_s.start()
    own_s = pltpu.make_async_copy(satt.at[my_rows, :], att6.at[:, my_lanes], loc_sem.at[2])
    own_s.start()

    def wait_parts(j, carry):
        at = lax.rem(me + NF - j, NF)
        rdma(stage.at[at], recv.at[at], a_send.at[at], a_recv.at[at], {"frame": at}).wait_recv()
        return carry

    lax.fori_loop(1, NF, wait_parts, 0)

    span = NF * ROWS
    same = (
        lax.broadcasted_iota(jnp.int32, (span, span), 0) % ROWS
        == lax.broadcasted_iota(jnp.int32, (span, span), 1) % ROWS
    )

    def temporal(t, carry):
        q = recv[:, t, 0].reshape(span, HD)
        k = recv[:, t, 1].reshape(span, HD)
        v = recv[:, t, 2].reshape(span, HD)
        s = jnp.where(same, dot_t(q, k) * SCALE, -1e30)
        e = jnp.exp(s - jnp.max(s, axis=-1, keepdims=True))
        norm = jnp.sum(e, axis=-1, keepdims=True)
        o = dot(e.astype(jnp.bfloat16), v) / norm
        ostage[:, t] = o.astype(jnp.bfloat16).reshape(NF, ROWS, HD)
        return carry

    lax.fori_loop(0, slots, temporal, 0)

    def send_back(j, carry):
        to = lax.rem(me + j, NF)
        rdma(ostage.at[to], oret.at[me], o_send.at[to], o_recv.at[me], {"frame": to}).start()
        return carry

    lax.fori_loop(1, NF, send_back, 0)
    oret[pl.ds(me, 1)] = ostage[pl.ds(me, 1)]

    own_s.wait()
    rdma(
        satt.at[my_rows, :], att6.at[:, other_lanes], px_send.at[2], px_recv.at[2], partner
    ).wait_recv()
    own_w.wait()
    rdma(
        weight, wfull.at[pl.ds(pl.multiple_of(other * WL, HD), WL), :],
        px_send.at[1], px_recv.at[1], partner,
    ).wait_recv()

    def wait_back(j, carry):
        at = lax.rem(me + NF - j, NF)
        rdma(ostage.at[at], oret.at[at], o_send.at[at], o_recv.at[at], {"frame": at}).wait_recv()
        return carry

    lax.fori_loop(1, NF, wait_back, 0)

    for h in range(HC):
        lanes = slice(h * HD, (h + 1) * HD)
        is_temporal = kinds[y * HC + h] == 1
        att[:, lanes] = jnp.where(
            is_temporal, oret[:, h].reshape(HALF, HD), att6[:, lanes]
        )

    def product(block, half):
        start = pl.multiple_of(block * WC + half * WL, HD)
        return dot(att[...], wfull[:, pl.ds(start, WL)])

    up, down, far = lax.rem(y + 1, NY), lax.rem(y + NY - 1, NY), lax.rem(y + 2, NY)
    sends = []

    def send(src, dst, index, who):
        copy = rdma(src, dst, y_send.at[index], y_recv.at[index], who)
        copy.start()
        sends.append(copy)

    far_out[0] = product(far, 0).astype(jnp.bfloat16)
    send(far_out.at[0], far_in.at[0], 0, plus)
    far_out[1] = product(far, 1).astype(jnp.bfloat16)
    send(far_out.at[1], far_in.at[1], 1, minus)
    near_out[0, 1] = product(up, 1).astype(jnp.bfloat16)
    send(near_out.at[0, 1], near_in.at[0, 1], 2, plus)
    near_out[1, 0] = product(down, 0).astype(jnp.bfloat16)
    send(near_out.at[1, 0], near_in.at[1, 0], 3, minus)
    up_part = product(up, 0)
    sends[0].wait_recv()
    near_out[0, 0] = (up_part + far_in[0].astype(jnp.float32)).astype(jnp.bfloat16)
    send(near_out.at[0, 0], near_in.at[0, 0], 4, plus)
    down_part = product(down, 1)
    sends[1].wait_recv()
    near_out[1, 1] = (down_part + far_in[1].astype(jnp.float32)).astype(jnp.bfloat16)
    send(near_out.at[1, 1], near_in.at[1, 1], 5, minus)

    for index in range(2, 6):
        sends[index].wait_recv()

    def total(half):
        return (
            product(y, half)
            + near_in[0, half].astype(jnp.float32)
            + near_in[1, half].astype(jnp.float32)
        ).astype(jnp.bfloat16)

    swap_out[...] = total(other)
    last = rdma(swap_out, out.at[my_rows, :], px_send.at[3], px_recv.at[3], partner)
    last.start()
    out[my_rows, :] = total(c)
    rdma(swap_out, out.at[other_rows, :], px_send.at[3], px_recv.at[3], partner).wait_recv()

    swap.wait_send()
    swap_w.wait_send()
    swap_s.wait_send()
    last.wait_send()
    for copy in sends:
        copy.wait_send()

    def drain(j, carry):
        to = lax.rem(me + j, NF)
        rdma(stage.at[to], recv.at[me], a_send.at[to], a_recv.at[me], {"frame": to}).wait_send()
        rdma(ostage.at[to], oret.at[me], o_send.at[to], o_recv.at[me], {"frame": to}).wait_send()
        return carry

    lax.fori_loop(1, NF, drain, 0)

    def drain_z(j, carry):
        to = lax.rem(z + j, NZ)
        rdma(
            kv0.at[:, z, x], kv0.at[:, z, x], z_send.at[to], z_recv.at[z], {"frame": to * NX + x}
        ).wait_send()
        return carry

    lax.fori_loop(1, NZ, drain_z, 0)

    def drain_x(j, carry):
        to = lax.rem(x + j, NX)
        rdma(
            kv0.at[:, :, x], kv0.at[:, :, x], x_send.at[to], x_recv.at[x], {"frame": z * NX + to}
        ).wait_send()
        return carry

    lax.fori_loop(1, NX, drain_x, 0)

    @pl.when(me == 0)
    def _():
        def drain_s(j, carry):
            rows = pl.ds(pl.multiple_of(j * CH, CH), CH)
            rdma(
                qkv.at[pl.ds(1, 2), rows, :], kv0.at[:, j // NX, j % NX],
                sc_send.at[j], sc_recv, {"frame": j},
            ).wait_send()
            return carry

        lax.fori_loop(1, NF, drain_s, 0)


def attention(slots, kinds, qkv, weight):
    bf = jnp.bfloat16
    vmem = pl.BlockSpec(memory_space=pltpu.VMEM)
    dma = pltpu.SemaphoreType.DMA
    return pl.pallas_call(
        functools.partial(kernel, slots),
        out_shape=jax.ShapeDtypeStruct((TOK, WL), bf),
        in_specs=[pl.BlockSpec(memory_space=pltpu.SMEM), vmem, vmem],
        out_specs=vmem,
        scratch_shapes=[
            pltpu.VMEM((3, HALF, WC), bf),
            pltpu.VMEM((NF, slots, 3, ROWS, HD), bf),
            pltpu.VMEM((NF, slots, 3, ROWS, HD), bf),
            pltpu.VMEM((NF, slots, ROWS, HD), bf),
            pltpu.VMEM((NF, slots, ROWS, HD), bf),
            pltpu.VMEM((2, NZ, NX, CH, WL), bf),
            pltpu.VMEM((TOK, WL), bf),
            pltpu.VMEM((HALF, WC), bf),
            pltpu.VMEM((HALF, WC), bf),
            pltpu.VMEM((WC, NY * WC), bf),
            pltpu.VMEM((2, HALF, WL), bf),
            pltpu.VMEM((2, HALF, WL), bf),
            pltpu.VMEM((2, 2, HALF, WL), bf),
            pltpu.VMEM((2, 2, HALF, WL), bf),
            pltpu.VMEM((HALF, WL), bf),
            dma((3,)),
            dma((4,)), dma((4,)),
            dma((NF,)), dma((NF,)),
            dma((NF,)), dma((NF,)),
            dma((NF,)), dma,
            dma((NZ,)), dma((NZ,)),
            dma((NX,)), dma((NX,)),
            dma((6,)), dma((6,)),
        ],
        compiler_params=pltpu.CompilerParams(
            collective_id=slots, has_side_effects=True, vmem_limit_bytes=56 * 1024 * 1024
        ),
    )(kinds, qkv, weight)


def local(qkv, head_kinds, out_weight):
    return attention(HC, head_kinds, qkv.transpose(1, 0, 2), out_weight)


def solution(mesh):
    placed = (P("frame", None, "head"), P(), P("head", None))
    return jax.shard_map(
        local, mesh=mesh, in_specs=placed, out_specs=P("frame", "head"), check_vma=False
    )
```

```python
import functools

import jax
import jax.numpy as jnp
from jax import lax
from jax.experimental import pallas as pl
from jax.experimental.pallas import tpu as pltpu
from jax.sharding import PartitionSpec as P

HD = 128
MESH = pl.DeviceIdType.MESH
NX = 4
NZ = 8
NF = NX * NZ
NY = 4
HL = 3
HC = 2 * HL
TOK = 1024
HALF = TOK // 2
ROWS = HALF // NF
CH = TOK // NF
WL = HL * HD
WC = HC * HD
QB = 256
PB = 128
SLOTS = (3, 4, 5, 6)
GAIN = HD ** -0.5 * 1.4426950408889634


def rdma(src, dst, send_sem, recv_sem, where):
    return pltpu.make_async_remote_copy(
        src_ref=src, dst_ref=dst, send_sem=send_sem, recv_sem=recv_sem,
        device_id=where, device_id_type=MESH,
    )


def dot_t(a, b):
    return lax.dot_general(a, b, (((1,), (1,)), ((), ())), preferred_element_type=jnp.float32)


def dot(a, b):
    return jnp.dot(a, b, preferred_element_type=jnp.float32)


def kernel(
    slots, kinds, qkv_in, weight, out,
    qkv, run_max, run_norm, run_mix, qkv6, stage, recv, ostage, oret, kv0, satt, att6, att, wfull,
    far_out, far_in, near_out, near_in, swap_out,
    loc_sem, px_send, px_recv, a_send, a_recv, o_send, o_recv,
    sc_send, sc_recv, zu_send, zd_send, z_recv, x_send, x_recv, y_send, y_recv,
):
    me = lax.axis_index("frame")
    mh = lax.axis_index("head")
    z, x = me // NX, me % NX
    y, c = mh // 2, mh % 2
    other = 1 - c
    partner = {"head": y * 2 + other}
    plus = {"head": lax.rem(y + 1, NY) * 2 + c}
    minus = {"head": lax.rem(y + NY - 1, NY) * 2 + c}

    barrier = pltpu.get_barrier_semaphore()

    def greet(j, carry):
        pl.semaphore_signal(
            barrier, inc=1, device_id={"frame": lax.rem(me + j, NF)}, device_id_type=MESH
        )
        return carry

    lax.fori_loop(1, NF, greet, 0)
    for who in (partner, plus, minus):
        pl.semaphore_signal(barrier, inc=1, device_id=who, device_id_type=MESH)

    my_rows = pl.ds(pl.multiple_of(c * HALF, HALF), HALF)
    other_rows = pl.ds(pl.multiple_of(other * HALF, HALF), HALF)
    my_lanes = pl.ds(pl.multiple_of(c * WL, HD), WL)
    other_lanes = pl.ds(pl.multiple_of(other * WL, HD), WL)
    my_wrows = pl.ds(pl.multiple_of(c * WL, HD), WL)

    load = pltpu.make_async_copy(qkv_in, qkv, loc_sem.at[3])
    load.start()
    own_qkv = pltpu.make_async_copy(
        qkv_in.at[:, my_rows, :], qkv6.at[:, :, my_lanes], loc_sem.at[0]
    )
    own_qkv.start()
    own_w = pltpu.make_async_copy(weight, wfull.at[my_wrows, :], loc_sem.at[1])
    own_w.start()

    load.wait()

    def own_frame(n, carry):
        h = n // (TOK // QB)
        rows = pl.ds(pl.multiple_of(n % (TOK // QB) * QB, QB), QB)
        lanes = pl.ds(pl.multiple_of(h * HD, HD), HD)
        s = dot_t(qkv[0, rows, lanes], qkv[1, :, lanes])
        top = jnp.max(s, axis=-1, keepdims=True)
        e = jnp.exp2((s - top) * GAIN)
        run_max[h, rows] = top
        run_norm[h, rows] = jnp.sum(e, axis=-1, keepdims=True)
        run_mix[rows, lanes] = dot(e.astype(jnp.bfloat16), qkv[2, :, lanes])
        return carry

    lax.fori_loop(0, HL * (TOK // QB), own_frame, 0)

    pl.semaphore_wait(barrier, NF - 1 + 3)

    swap = rdma(
        qkv_in.at[:, other_rows, :], qkv6.at[:, :, my_lanes], px_send.at[0], px_recv.at[0], partner
    )
    swap.start()

    @pl.when(me == 0)
    def _():
        own_chunk = pltpu.make_async_copy(
            qkv_in.at[pl.ds(1, 2), pl.ds(0, CH), :], kv0.at[:, 0, 0], sc_recv
        )
        own_chunk.start()

        def scatter(j, carry):
            rows = pl.ds(pl.multiple_of(j * CH, CH), CH)
            rdma(
                qkv_in.at[pl.ds(1, 2), rows, :], kv0.at[:, j // NX, j % NX],
                sc_send.at[j], sc_recv, {"frame": j},
            ).start()
            return carry

        lax.fori_loop(1, NF, scatter, 0)

    own_qkv.wait()
    rdma(
        qkv.at[:, my_rows, :], qkv6.at[:, :, other_lanes], px_send.at[0], px_recv.at[0], partner
    ).wait_recv()

    kind = [kinds[y * HC + h] for h in range(HC)]
    place = [0]
    for h in range(HC - 1):
        place.append(place[-1] + kind[h])
    for t in range(slots):
        for i in range(3):
            part = qkv6[i, :, t * HD : (t + 1) * HD]
            if slots < HC:
                for h in range(t + 1, HC):
                    here = (kind[h] == 1) & (place[h] == t)
                    part = jnp.where(here, qkv6[i, :, h * HD : (h + 1) * HD], part)
            stage[:, t, i] = part.reshape(NF, ROWS, HD)

    pltpu.make_async_copy(
        qkv.at[pl.ds(1, 2), pl.ds(0, CH), :], kv0.at[:, z, x], sc_recv
    ).wait()

    z_up = {"frame": lax.rem(z + 1, NZ) * NX + x}
    z_down = {"frame": lax.rem(z + NZ - 1, NZ) * NX + x}
    x_up = {"frame": z * NX + lax.rem(x + 1, NX)}
    x_down = {"frame": z * NX + lax.rem(x + NX - 1, NX)}
    x_far = {"frame": z * NX + lax.rem(x + 2, NX)}
    ring = []

    def pass_on(src, send_sem, recv_sem, who):
        copy = rdma(src, src, send_sem, recv_sem, who)
        copy.start()
        ring.append(copy)

    def arrived(part, recv_sem):
        rdma(part, part, zu_send.at[0, 0], recv_sem, z_up).wait_recv()

    def z_part(at, h):
        return kv0.at[:, at, x, :, h * HD : (h + 1) * HD]

    def x_part(at, h):
        return kv0.at[:, :, at, :, h * HD : (h + 1) * HD]

    for step in range(NZ // 2):
        low = lax.rem(z + NZ - step, NZ)
        high = lax.rem(z + step, NZ)
        for h in range(HL):
            if step > 0:
                arrived(z_part(low, h), z_recv.at[h, low])
            pass_on(z_part(low, h), zu_send.at[h, step], z_recv.at[h, low], z_up)
            if step < NZ // 2 - 1:
                if step > 0:
                    arrived(z_part(high, h), z_recv.at[h, high])
                pass_on(z_part(high, h), zd_send.at[h, step], z_recv.at[h, high], z_down)
    for h in range(HL):
        for at in (lax.rem(z + NZ // 2, NZ), lax.rem(z + NZ // 2 - 1, NZ)):
            arrived(z_part(at, h), z_recv.at[h, at])
        for j, who in enumerate((x_far, x_up, x_down)):
            pass_on(x_part(x, h), x_send.at[h, j], x_recv.at[h, x], who)

    def send_parts(j, carry):
        to = lax.rem(me + j, NF)
        rdma(stage.at[to], recv.at[me], a_send.at[to], a_recv.at[me], {"frame": to}).start()
        return carry

    lax.fori_loop(1, NF, send_parts, 0)
    recv[pl.ds(me, 1)] = stage[pl.ds(me, 1)]

    swap_w = rdma(weight, wfull.at[my_wrows, :], px_send.at[1], px_recv.at[1], partner)
    swap_w.start()


    def wait_parts(j, carry):
        at = lax.rem(me + NF - j, NF)
        rdma(stage.at[at], recv.at[at], a_send.at[at], a_recv.at[at], {"frame": at}).wait_recv()
        return carry

    lax.fori_loop(1, NF, wait_parts, 0)

    span = NF * ROWS
    same = (
        lax.broadcasted_iota(jnp.int32, (span, span), 0) % ROWS
        == lax.broadcasted_iota(jnp.int32, (span, span), 1) % ROWS
    )

    def temporal(t, carry):
        q = recv[:, t, 0].reshape(span, HD)
        k = recv[:, t, 1].reshape(span, HD)
        v = recv[:, t, 2].reshape(span, HD)
        s = jnp.where(same, dot_t(q, k), -1e30)
        e = jnp.exp2((s - jnp.max(s, axis=-1, keepdims=True)) * GAIN)
        norm = jnp.sum(e, axis=-1, keepdims=True)
        o = dot(e.astype(jnp.bfloat16), v) / norm
        ostage[:, t] = o.astype(jnp.bfloat16).reshape(NF, ROWS, HD)
        return carry

    lax.fori_loop(0, slots, temporal, 0)

    def send_back(j, carry):
        to = lax.rem(me + j, NF)
        rdma(ostage.at[to], oret.at[me], o_send.at[to], o_recv.at[me], {"frame": to}).start()
        return carry

    lax.fori_loop(1, NF, send_back, 0)
    oret[pl.ds(me, 1)] = ostage[pl.ds(me, 1)]


    def wait_x(n, carry):
        h, j = n // (NX - 1), n % (NX - 1) + 1
        at = lax.rem(x + j, NX)
        part = kv0.at[:, :, at, :, pl.ds(pl.multiple_of(h * HD, HD), HD)]
        arrived(part, x_recv.at[h, at])
        return carry

    lax.fori_loop(0, HL * (NX - 1), wait_x, 0)

    def first_frame(n, carry):
        h = n // (TOK // QB)
        rows = pl.ds(pl.multiple_of(n % (TOK // QB) * QB, QB), QB)
        lanes = pl.ds(pl.multiple_of(h * HD, HD), HD)
        s = dot_t(qkv[0, rows, lanes], kv0[0, :, :, :, lanes].reshape(TOK, HD))
        s = jnp.where(me == 0, -1e30, s)
        before = run_max[h, rows]
        top = jnp.maximum(before, jnp.max(s, axis=-1, keepdims=True))
        keep = jnp.exp2((before - top) * GAIN)
        e = jnp.exp2((s - top) * GAIN)
        norm = run_norm[h, rows] * keep + jnp.sum(e, axis=-1, keepdims=True)
        mixed = run_mix[rows, lanes] * keep + dot(
            e.astype(jnp.bfloat16), kv0[1, :, :, :, lanes].reshape(TOK, HD)
        )
        satt[rows, lanes] = (mixed / norm).astype(jnp.bfloat16)
        return carry

    lax.fori_loop(0, HL * (TOK // QB), first_frame, 0)

    swap_s = rdma(
        satt.at[other_rows, :], att6.at[:, my_lanes], px_send.at[2], px_recv.at[2], partner
    )
    swap_s.start()
    own_s = pltpu.make_async_copy(satt.at[my_rows, :], att6.at[:, my_lanes], loc_sem.at[2])
    own_s.start()

    own_s.wait()
    rdma(
        satt.at[my_rows, :], att6.at[:, other_lanes], px_send.at[2], px_recv.at[2], partner
    ).wait_recv()
    own_w.wait()
    rdma(
        weight, wfull.at[pl.ds(pl.multiple_of(other * WL, HD), WL), :],
        px_send.at[1], px_recv.at[1], partner,
    ).wait_recv()

    def wait_back(j, carry):
        at = lax.rem(me + NF - j, NF)
        rdma(ostage.at[at], oret.at[at], o_send.at[at], o_recv.at[at], {"frame": at}).wait_recv()
        return carry

    lax.fori_loop(1, NF, wait_back, 0)

    for h in range(HC):
        lanes = slice(h * HD, (h + 1) * HD)
        part = att6[:, lanes]
        for t in range(min(h + 1, slots)) if slots < HC else [h]:
            here = (kind[h] == 1) & (place[h] == t) if slots < HC else kind[h] == 1
            part = jnp.where(here, oret[:, t].reshape(HALF, HD), part)
        att[:, lanes] = part

    def product(dst, block, half, *more):
        lanes = pl.ds(pl.multiple_of(block * WC + half * WL, HD), WL)

        def piece(b, carry):
            rows = pl.ds(pl.multiple_of(b * PB, PB), PB)
            total = dot(att[rows, :], wfull[:, lanes])
            for extra in more:
                total += extra[rows, :].astype(jnp.float32)
            dst[rows, :] = total.astype(jnp.bfloat16)
            return carry

        lax.fori_loop(0, HALF // PB, piece, 0)

    up, down, far = lax.rem(y + 1, NY), lax.rem(y + NY - 1, NY), lax.rem(y + 2, NY)
    sends = []

    def send(src, dst, index, who):
        copy = rdma(src, dst, y_send.at[index], y_recv.at[index], who)
        copy.start()
        sends.append(copy)

    product(far_out.at[0], far, 0)
    send(far_out.at[0], far_in.at[0], 0, plus)
    product(far_out.at[1], far, 1)
    send(far_out.at[1], far_in.at[1], 1, minus)
    product(near_out.at[0, 1], up, 1)
    send(near_out.at[0, 1], near_in.at[0, 1], 2, plus)
    product(near_out.at[1, 0], down, 0)
    send(near_out.at[1, 0], near_in.at[1, 0], 3, minus)
    sends[0].wait_recv()
    product(near_out.at[0, 0], up, 0, far_in.at[0])
    send(near_out.at[0, 0], near_in.at[0, 0], 4, plus)
    sends[1].wait_recv()
    product(near_out.at[1, 1], down, 1, far_in.at[1])
    send(near_out.at[1, 1], near_in.at[1, 1], 5, minus)

    for index in range(2, 6):
        sends[index].wait_recv()

    product(swap_out, y, other, near_in.at[0, other], near_in.at[1, other])
    last = rdma(swap_out, out.at[my_rows, :], px_send.at[3], px_recv.at[3], partner)
    last.start()
    product(out.at[my_rows, :], y, c, near_in.at[0, c], near_in.at[1, c])
    rdma(swap_out, out.at[other_rows, :], px_send.at[3], px_recv.at[3], partner).wait_recv()

    swap.wait_send()
    swap_w.wait_send()
    swap_s.wait_send()
    last.wait_send()
    for copy in sends:
        copy.wait_send()

    def drain(j, carry):
        to = lax.rem(me + j, NF)
        rdma(stage.at[to], recv.at[me], a_send.at[to], a_recv.at[me], {"frame": to}).wait_send()
        rdma(ostage.at[to], oret.at[me], o_send.at[to], o_recv.at[me], {"frame": to}).wait_send()
        return carry

    lax.fori_loop(1, NF, drain, 0)

    for copy in ring:
        copy.wait_send()

    @pl.when(me == 0)
    def _():
        def drain_s(j, carry):
            rows = pl.ds(pl.multiple_of(j * CH, CH), CH)
            rdma(
                qkv_in.at[pl.ds(1, 2), rows, :], kv0.at[:, j // NX, j % NX],
                sc_send.at[j], sc_recv, {"frame": j},
            ).wait_send()
            return carry

        lax.fori_loop(1, NF, drain_s, 0)


def attention(slots, kinds, qkv, weight):
    bf = jnp.bfloat16
    vmem = pl.BlockSpec(memory_space=pltpu.VMEM)
    hbm = pl.BlockSpec(memory_space=pl.ANY)
    dma = pltpu.SemaphoreType.DMA
    return pl.pallas_call(
        functools.partial(kernel, slots),
        out_shape=jax.ShapeDtypeStruct((TOK, WL), bf),
        in_specs=[pl.BlockSpec(memory_space=pltpu.SMEM), hbm, hbm],
        out_specs=vmem,
        scratch_shapes=[
            pltpu.VMEM((3, TOK, WL), bf),
            pltpu.VMEM((HL, TOK, 1), jnp.float32),
            pltpu.VMEM((HL, TOK, 1), jnp.float32),
            pltpu.VMEM((TOK, WL), jnp.float32),
            pltpu.VMEM((3, HALF, WC), bf),
            pltpu.VMEM((NF, slots, 3, ROWS, HD), bf),
            pltpu.VMEM((NF, slots, 3, ROWS, HD), bf),
            pltpu.VMEM((NF, slots, ROWS, HD), bf),
            pltpu.VMEM((NF, slots, ROWS, HD), bf),
            pltpu.VMEM((2, NZ, NX, CH, WL), bf),
            pltpu.VMEM((TOK, WL), bf),
            pltpu.VMEM((HALF, WC), bf),
            pltpu.VMEM((HALF, WC), bf),
            pltpu.VMEM((WC, NY * WC), bf),
            pltpu.VMEM((2, HALF, WL), bf),
            pltpu.VMEM((2, HALF, WL), bf),
            pltpu.VMEM((2, 2, HALF, WL), bf),
            pltpu.VMEM((2, 2, HALF, WL), bf),
            pltpu.VMEM((HALF, WL), bf),
            dma((4,)),
            dma((4,)), dma((4,)),
            dma((NF,)), dma((NF,)),
            dma((NF,)), dma((NF,)),
            dma((NF,)), dma,
            dma((HL, NZ)), dma((HL, NZ)), dma((HL, NZ)),
            dma((HL, NX)), dma((HL, NX)),
            dma((6,)), dma((6,)),
        ],
        compiler_params=pltpu.CompilerParams(
            collective_id=slots, has_side_effects=True, vmem_limit_bytes=56 * 1024 * 1024
        ),
    )(kinds, qkv, weight)


def local(qkv, head_kinds, out_weight):
    most = jnp.max(jnp.sum(
        jnp.where(jnp.arange(NY * HC) // HC == jnp.arange(NY)[:, None], head_kinds, 0), axis=1
    ))
    choices = [functools.partial(attention, slots) for slots in SLOTS]
    return lax.switch(
        jnp.clip(most - SLOTS[0], 0, len(SLOTS) - 1),
        choices, head_kinds, qkv.transpose(1, 0, 2), out_weight,
    )


def solution(mesh):
    placed = (P("frame", None, "head"), P(), P("head", None))
    return jax.shard_map(
        local, mesh=mesh, in_specs=placed, out_specs=P("frame", "head"), check_vma=False
    )
```

```python
import functools

import jax
import jax.numpy as jnp
from jax import lax
from jax.experimental import pallas as pl
from jax.experimental.pallas import tpu as pltpu
from jax.sharding import PartitionSpec as P

HD = 128
MESH = pl.DeviceIdType.MESH
NX = 4
NZ = 8
NF = NX * NZ
NY = 4
HL = 3
HC = 2 * HL
TOK = 1024
HALF = TOK // 2
ROWS = HALF // NF
PART = ROWS // 2
CH = TOK // NF
WL = HL * HD
WC = HC * HD
QB = 256
PB = 128
NP = PB // ROWS
SIZES = ((4, 4), (4, 5), (5, 4), (5, 5), (HC, HC))
GAIN = HD ** -0.5 * 1.4426950408889634


def rdma(src, dst, send_sem, recv_sem, where):
    return pltpu.make_async_remote_copy(
        src_ref=src, dst_ref=dst, send_sem=send_sem, recv_sem=recv_sem,
        device_id=where, device_id_type=MESH,
    )


def dot_t(a, b):
    return lax.dot_general(a, b, (((1,), (1,)), ((), ())), preferred_element_type=jnp.float32)


def dot(a, b):
    return jnp.dot(a, b, preferred_element_type=jnp.float32)


def kernel(
    slots, frees, kinds, qkv_in, weight, out,
    qkv6, kv_other, stage, recv, ostage, oret, kvst, kv0, kv1, sel, satt, att6, att, wfull,
    far_out, far_in, near_out, near_in, swap_out, swap_in, mine,
    loc_sem, px_send, px_recv, a_send, a_recv, o_send, o_recv,
    sc_send, sc_recv, zu_send, zd_send, z_recv, x_send, x_recv, y_send, y_recv,
):
    me = lax.axis_index("frame")
    mh = lax.axis_index("head")
    z, x = me // NX, me % NX
    y, c = mh // 2, mh % 2
    other = 1 - c
    partner = {"head": y * 2 + other}
    plus = {"head": lax.rem(y + 1, NY) * 2 + c}
    minus = {"head": lax.rem(y + NY - 1, NY) * 2 + c}

    barrier = pltpu.get_barrier_semaphore()

    def greet(j, carry):
        pl.semaphore_signal(
            barrier, inc=1, device_id={"frame": lax.rem(me + j, NF)}, device_id_type=MESH
        )
        return carry

    lax.fori_loop(1, NF, greet, 0)
    for who in (partner, plus, minus):
        pl.semaphore_signal(barrier, inc=1, device_id=who, device_id_type=MESH)

    my_rows = pl.ds(pl.multiple_of(c * HALF, HALF), HALF)
    other_rows = pl.ds(pl.multiple_of(other * HALF, HALF), HALF)
    my_lanes = pl.ds(pl.multiple_of(c * WL, HD), WL)
    other_lanes = pl.ds(pl.multiple_of(other * WL, HD), WL)
    my_wrows = pl.ds(pl.multiple_of(c * WL, HD), WL)

    own_qkv = pltpu.make_async_copy(
        qkv_in.at[:, my_rows, :], qkv6.at[:, :, my_lanes], loc_sem.at[0]
    )
    own_qkv.start()
    own_w = pltpu.make_async_copy(weight, wfull.at[my_wrows, :], loc_sem.at[1])
    own_w.start()

    own_kv = pltpu.make_async_copy(
        qkv_in.at[pl.ds(1, 2), other_rows, :], kv_other.at[:, :, my_lanes], loc_sem.at[2]
    )
    own_kv.start()

    pl.semaphore_wait(barrier, NF - 1 + 3)

    swap = rdma(
        qkv_in.at[:, other_rows, :], qkv6.at[:, :, my_lanes], px_send.at[0], px_recv.at[0], partner
    )
    swap.start()

    own_qkv.wait()
    rdma(
        qkv_in.at[:, my_rows, :], qkv6.at[:, :, other_lanes], px_send.at[0], px_recv.at[0], partner
    ).wait_recv()

    kind = [kinds[y * HC + h] for h in range(HC)]
    place = [0]
    for h in range(HC - 1):
        place.append(place[-1] + kind[h])
    free = [h - place[h] for h in range(HC)]

    def chosen(ref, i, rows, wanted, place_of, slot, low):
        part = ref[i, rows, low * HD : (low + 1) * HD]
        for h in range(low + 1, HC):
            here = (kind[h] == wanted) & (place_of[h] == slot)
            part = jnp.where(here, ref[i, rows, h * HD : (h + 1) * HD], part)
        return part

    def in_pieces(body):
        def step(b, carry):
            body(b, pl.ds(pl.multiple_of(b * PB, PB), PB))
            return carry

        lax.fori_loop(0, HALF // PB, step, 0)

    @pl.when(me == 0)
    def _():
        def fill_first(b, rows):
            for n in range(frees):
                for i in range(2):
                    part = chosen(qkv6, 1 + i, rows, 0, free, n, n)
                    kvst[pl.ds(b * NP, NP), n, i] = part.reshape(NP, ROWS, HD)

        in_pieces(fill_first)
        pltpu.make_async_copy(kvst.at[0], kv0.at[0, 0], sc_recv).start()

        def scatter(j, carry):
            rdma(
                kvst.at[j], kv0.at[j // NX, j % NX], sc_send.at[j], sc_recv, {"frame": j}
            ).start()
            return carry

        lax.fori_loop(1, NF, scatter, 0)

    def fill_stage(b, rows):
        for t in range(slots):
            for i in range(3):
                part = chosen(qkv6, i, rows, 1, place, t, t)
                stage[pl.ds(b * NP, NP), t, i] = part.reshape(NP, ROWS, HD)

    in_pieces(fill_stage)

    def send_part(dz, dx):
        to = lax.rem(z + dz, NZ) * NX + lax.rem(x + dx, NX)
        rdma(stage.at[to], recv.at[me], a_send.at[to], a_recv.at[me], {"frame": to}).start()

    def turn(n):
        odd = lax.rem(n, 2)
        return odd * ((n + 1) // 2) + (1 - odd) * (NZ - n // 2)

    def send_straight(n, carry):
        send_part(turn(n), 0)
        return carry

    def send_row(n, carry):
        send_part(0, n)
        return carry

    def send_rest(n, carry):
        send_part(turn(n // (NX - 1) + 1), n % (NX - 1) + 1)
        return carry

    pltpu.make_async_copy(kvst.at[0], kv0.at[z, x], sc_recv).wait()

    z_up = {"frame": lax.rem(z + 1, NZ) * NX + x}
    z_down = {"frame": lax.rem(z + NZ - 1, NZ) * NX + x}
    x_up = {"frame": z * NX + lax.rem(x + 1, NX)}
    x_down = {"frame": z * NX + lax.rem(x + NX - 1, NX)}
    ring = []

    def pass_on(src, send_sem, recv_sem, who):
        copy = rdma(src, src, send_sem, recv_sem, who)
        copy.start()
        ring.append(copy)

    def arrived(part, recv_sem):
        rdma(part, part, zu_send.at[0], recv_sem, z_up).wait_recv()

    for step in range(NZ // 2):
        low = lax.rem(z + NZ - step, NZ)
        high = lax.rem(z + step, NZ)
        if step > 0:
            arrived(kv0.at[low, x], z_recv.at[low])
        pass_on(kv0.at[low, x], zu_send.at[step], z_recv.at[low], z_up)
        if step < NZ // 2 - 1:
            if step > 0:
                arrived(kv0.at[high, x], z_recv.at[high])
            pass_on(kv0.at[high, x], zd_send.at[step], z_recv.at[high], z_down)
    for at in (lax.rem(z + NZ // 2, NZ), lax.rem(z + NZ // 2 - 1, NZ)):
        arrived(kv0.at[at, x], z_recv.at[at])
    x_low, x_high = lax.rem(x + NX - 1, NX), lax.rem(x + 1, NX)
    x_over = lax.rem(x + 2, NX)
    pass_on(kv0.at[:, x], x_send.at[0], x_recv.at[x], x_up)
    pass_on(kv0.at[:, x], x_send.at[1], x_recv.at[x], x_down)

    lax.fori_loop(1, NZ, send_straight, 0)

    near_z, far_z = pl.ds(0, NZ // 2), pl.ds(NZ // 2, NZ // 2)
    arrived(kv0.at[:, x_low], x_recv.at[x_low])
    pass_on(kv0.at[near_z, x_low], x_send.at[2], x_recv.at[NX], x_up)
    arrived(kv0.at[:, x_high], x_recv.at[x_high])
    pass_on(kv0.at[far_z, x_high], x_send.at[3], x_recv.at[NX + 1], x_down)
    arrived(kv0.at[near_z, x_over], x_recv.at[NX])
    arrived(kv0.at[far_z, x_over], x_recv.at[NX + 1])
    share_first = rdma(kv0, kv1, px_send.at[2], px_recv.at[2], partner)
    share_first.start()
    share_kv = rdma(
        qkv_in.at[pl.ds(1, 2), my_rows, :], kv_other.at[:, :, my_lanes],
        px_send.at[5], px_recv.at[5], partner,
    )
    share_kv.start()
    lax.fori_loop(1, NX, send_row, 0)
    lax.fori_loop(0, (NZ - 1) * (NX - 1), send_rest, 0)
    recv[pl.ds(me, 1)] = stage[pl.ds(me, 1)]

    swap_w = rdma(weight, wfull.at[my_wrows, :], px_send.at[1], px_recv.at[1], partner)
    swap_w.start()


    own_kv.wait()
    share_first.wait_recv()
    rdma(
        qkv_in.at[pl.ds(1, 2), my_rows, :], kv_other.at[:, :, other_lanes],
        px_send.at[5], px_recv.at[5], partner,
    ).wait_recv()

    def spatial(n, carry):
        def select(b, rows):
            for at, (ref, i) in enumerate(
                ((qkv6, 0), (qkv6, 1), (kv_other, 0), (qkv6, 2), (kv_other, 1))
            ):
                sel[at, rows, :] = chosen(ref, i, rows, 0, free, n, 0)

        in_pieces(select)

        def block(b, inner):
            rows = pl.ds(pl.multiple_of(b * QB, QB), QB)
            q = sel[0, rows, :]
            firsts = [ref[:, :, n, 0].reshape(HALF, HD) for ref in (kv0, kv1)]
            scores = [dot_t(q, sel[1]), dot_t(q, sel[2])]
            scores += [jnp.where(me == 0, -1e30, dot_t(q, keys)) for keys in firsts]
            top = functools.reduce(
                jnp.maximum, [jnp.max(s, axis=-1, keepdims=True) for s in scores]
            )
            values = [sel[3], sel[4]] + [ref[:, :, n, 1].reshape(HALF, HD) for ref in (kv0, kv1)]
            norm, mixed = 0.0, 0.0
            for s, v in zip(scores, values):
                e = jnp.exp2((s - top) * GAIN)
                norm += jnp.sum(e, axis=-1, keepdims=True)
                mixed += dot(e.astype(jnp.bfloat16), v)
            satt[n, rows, :] = (mixed / norm).astype(jnp.bfloat16)
            return inner

        return lax.fori_loop(0, HALF // QB, block, carry)

    lax.fori_loop(0, frees, spatial, 0)

    def rows_of(tile, k):
        wide = tile.astype(jnp.float32)
        return wide[:, k * PART : (k + 1) * PART].reshape(-1, HD)

    def order(b, rows):
        for h in range(HC):
            part = satt[0, rows, :]
            for n in range(1, min(h + 1, frees)):
                part = jnp.where(free[h] == n, satt[n, rows, :], part)
            for k in range(2):
                att6[k, pl.ds(pl.multiple_of(b * PB // 2, PB // 2), PB // 2), h * HD : (h + 1) * HD] = (
                    rows_of(part.reshape(NP, ROWS, HD), k).astype(jnp.bfloat16)
                )

    in_pieces(order)
    own_w.wait()
    rdma(
        weight, wfull.at[pl.ds(pl.multiple_of(other * WL, HD), WL), :],
        px_send.at[1], px_recv.at[1], partner,
    ).wait_recv()

    def wait_parts(j, carry):
        at = lax.rem(me + NF - j, NF)
        rdma(stage.at[at], recv.at[at], a_send.at[at], a_recv.at[at], {"frame": at}).wait_recv()
        return carry

    lax.fori_loop(1, NF, wait_parts, 0)

    span = NF * PART
    same = (
        lax.broadcasted_iota(jnp.int32, (span, span), 0) % PART
        == lax.broadcasted_iota(jnp.int32, (span, span), 1) % PART
    )

    def temporal(t, k):
        q, key, v = (rows_of(recv[:, t, i], k).astype(jnp.bfloat16) for i in range(3))
        s = jnp.where(same, dot_t(q, key), -1e30)
        e = jnp.exp2((s - jnp.max(s, axis=-1, keepdims=True)) * GAIN)
        norm = jnp.sum(e, axis=-1, keepdims=True)
        return (dot(e.astype(jnp.bfloat16), v) / norm).reshape(NF, PART, HD)

    def back(to, k):
        return rdma(
            ostage.at[to, k], oret.at[me, k], o_send.at[k, to], o_recv.at[k, me], {"frame": to}
        )

    for k in range(2):

        def pair(n, carry, k=k):
            both = [temporal(jnp.minimum(2 * n + i, slots - 1), k) for i in range(2)]
            ostage[:, k, n] = jnp.concatenate(both, axis=1).astype(jnp.bfloat16)
            return carry

        lax.fori_loop(0, (slots + 1) // 2, pair, 0)

        def send_back(j, carry, k=k):
            back(lax.rem(me + j, NF), k).start()
            return carry

        lax.fori_loop(1, NF, send_back, 0)
        oret[pl.ds(me, 1), k] = ostage[pl.ds(me, 1), k]

    def product(dst, k, block, half, *more):
        lanes = pl.ds(pl.multiple_of(block * WC + half * WL, HD), WL)

        def piece(b, carry):
            rows = pl.ds(pl.multiple_of(b * PB, PB), PB)
            total = dot(att[k, rows, :], wfull[:, lanes])
            for extra in more:
                total += extra[rows, :].astype(jnp.float32)
            dst[rows, :] = total.astype(jnp.bfloat16)
            return carry

        lax.fori_loop(0, span // PB, piece, 0)

    up, down, far = lax.rem(y + 1, NY), lax.rem(y + NY - 1, NY), lax.rem(y + 2, NY)

    def y_copy(k, index):
        parts = (
            (far_out.at[k, 0], far_in.at[k, 0], plus),
            (far_out.at[k, 1], far_in.at[k, 1], minus),
            (near_out.at[k, 0, 1], near_in.at[k, 0, 1], plus),
            (near_out.at[k, 1, 0], near_in.at[k, 1, 0], minus),
            (near_out.at[k, 0, 0], near_in.at[k, 0, 0], plus),
            (near_out.at[k, 1, 1], near_in.at[k, 1, 1], minus),
        )
        src, dst, who = parts[index]
        return rdma(src, dst, y_send.at[k, index], y_recv.at[k, index], who)

    def reduce_chunk(k, carry):
        def wait_back(j, inner):
            at = lax.rem(me + NF - j, NF)
            rdma(
                ostage.at[at, k], oret.at[at, k], o_send.at[k, at], o_recv.at[k, at],
                {"frame": at},
            ).wait_recv()
            return inner

        lax.fori_loop(1, NF, wait_back, 0)

        def gather(b, rows):
            half_rows = pl.ds(pl.multiple_of(b * PB // 2, PB // 2), PB // 2)
            for h in range(HC):
                lanes = slice(h * HD, (h + 1) * HD)
                part = att6[k, half_rows, lanes].astype(jnp.float32)
                for t in range(min(h + 1, slots)):
                    here = (kind[h] == 1) & (place[h] == t)
                    returned = rows_of(oret[pl.ds(b * NP, NP), k, t // 2], t % 2)
                    part = jnp.where(here, returned, part)
                att[k, half_rows, lanes] = part.astype(jnp.bfloat16)

        in_pieces(gather)

        product(far_out.at[k, 0], k, far, 0)
        y_copy(k, 0).start()
        product(far_out.at[k, 1], k, far, 1)
        y_copy(k, 1).start()
        product(near_out.at[k, 0, 1], k, up, 1)
        y_copy(k, 2).start()
        product(near_out.at[k, 1, 0], k, down, 0)
        y_copy(k, 3).start()
        y_copy(k, 0).wait_recv()
        product(near_out.at[k, 0, 0], k, up, 0, far_in.at[k, 0])
        y_copy(k, 4).start()
        y_copy(k, 1).wait_recv()
        product(near_out.at[k, 1, 1], k, down, 1, far_in.at[k, 1])
        y_copy(k, 5).start()
        return carry

    lax.fori_loop(0, 2, reduce_chunk, 0)

    def swap_copy(k):
        return rdma(
            swap_out.at[k], swap_in.at[k], px_send.at[3 + k], px_recv.at[3 + k], partner
        )

    def finish(k, carry):
        for index in range(2, 6):
            y_copy(k, index).wait_recv()
        product(swap_out.at[k], k, y, other, near_in.at[k, 0, other], near_in.at[k, 1, other])
        swap_copy(k).start()
        product(mine.at[k], k, y, c, near_in.at[k, 0, c], near_in.at[k, 1, c])
        return carry

    lax.fori_loop(0, 2, finish, 0)

    def join(src):
        tiles = [src[k].astype(jnp.float32).reshape(NF, PART, WL) for k in range(2)]
        return jnp.concatenate(tiles, axis=1).reshape(HALF, WL).astype(jnp.bfloat16)

    out[my_rows, :] = join(mine)
    for k in range(2):
        swap_copy(k).wait_recv()
    out[other_rows, :] = join(swap_in)

    swap.wait_send()
    swap_w.wait_send()
    share_first.wait_send()
    share_kv.wait_send()
    for k in range(2):
        swap_copy(k).wait_send()
        for index in range(6):
            y_copy(k, index).wait_send()

    def drain(j, carry):
        to = lax.rem(me + j, NF)
        rdma(stage.at[to], recv.at[me], a_send.at[to], a_recv.at[me], {"frame": to}).wait_send()
        back(to, 0).wait_send()
        back(to, 1).wait_send()
        return carry

    lax.fori_loop(1, NF, drain, 0)

    for copy in ring:
        copy.wait_send()

    @pl.when(me == 0)
    def _():
        def drain_s(j, carry):
            rdma(
                kvst.at[j], kv0.at[j // NX, j % NX], sc_send.at[j], sc_recv, {"frame": j}
            ).wait_send()
            return carry

        lax.fori_loop(1, NF, drain_s, 0)


def attention(slots, frees, ident, kinds, qkv, weight):
    bf = jnp.bfloat16
    vmem = pl.BlockSpec(memory_space=pltpu.VMEM)
    hbm = pl.BlockSpec(memory_space=pl.ANY)
    dma = pltpu.SemaphoreType.DMA
    return pl.pallas_call(
        functools.partial(kernel, slots, frees),
        out_shape=jax.ShapeDtypeStruct((TOK, WL), bf),
        in_specs=[pl.BlockSpec(memory_space=pltpu.SMEM), hbm, hbm],
        out_specs=vmem,
        scratch_shapes=[
            pltpu.VMEM((3, HALF, WC), bf),
            pltpu.VMEM((2, HALF, WC), bf),
            pltpu.VMEM((NF, slots, 3, ROWS, HD), bf),
            pltpu.VMEM((NF, slots, 3, ROWS, HD), bf),
            pltpu.VMEM((NF, 2, (slots + 1) // 2, ROWS, HD), bf),
            pltpu.VMEM((NF, 2, (slots + 1) // 2, ROWS, HD), bf),
            pltpu.VMEM((NF, frees, 2, ROWS, HD), bf),
            pltpu.VMEM((NZ, NX, frees, 2, ROWS, HD), bf),
            pltpu.VMEM((NZ, NX, frees, 2, ROWS, HD), bf),
            pltpu.VMEM((5, HALF, HD), bf),
            pltpu.VMEM((frees, HALF, HD), bf),
            pltpu.VMEM((2, HALF // 2, WC), bf),
            pltpu.VMEM((2, HALF // 2, WC), bf),
            pltpu.VMEM((WC, NY * WC), bf),
            pltpu.VMEM((2, 2, HALF // 2, WL), bf),
            pltpu.VMEM((2, 2, HALF // 2, WL), bf),
            pltpu.VMEM((2, 2, 2, HALF // 2, WL), bf),
            pltpu.VMEM((2, 2, 2, HALF // 2, WL), bf),
            pltpu.VMEM((2, HALF // 2, WL), bf),
            pltpu.VMEM((2, HALF // 2, WL), bf),
            pltpu.VMEM((2, HALF // 2, WL), bf),
            dma((4,)),
            dma((6,)), dma((6,)),
            dma((NF,)), dma((NF,)),
            dma((2, NF)), dma((2, NF)),
            dma((NF,)), dma,
            dma((NZ,)), dma((NZ,)), dma((NZ,)),
            dma((NX,)), dma((NX + 2,)),
            dma((2, 6)), dma((2, 6)),
        ],
        compiler_params=pltpu.CompilerParams(
            collective_id=ident, has_side_effects=True, vmem_limit_bytes=56 * 1024 * 1024
        ),
    )(kinds, qkv, weight)


def local(qkv, head_kinds, out_weight):
    chip = jnp.arange(NY * HC) // HC == jnp.arange(NY)[:, None]
    counts = jnp.sum(jnp.where(chip, head_kinds, 0), axis=1)
    most, least = jnp.max(counts), jnp.min(counts)
    choices = [
        functools.partial(attention, slots, frees, ident)
        for ident, (slots, frees) in enumerate(SIZES)
    ]
    fits = [(most <= slots) & (HC - least <= frees) for slots, frees in SIZES[:-1]]
    index = functools.reduce(
        lambda rest, n: jnp.where(fits[n], n, rest), reversed(range(len(fits))), len(fits)
    )
    return lax.switch(index, choices, head_kinds, qkv.transpose(1, 0, 2), out_weight)


def solution(mesh):
    placed = (P("frame", None, "head"), P(), P("head", None))
    return jax.shard_map(
        local, mesh=mesh, in_specs=placed, out_specs=P("frame", "head"), check_vma=False
    )
```

```python
import functools

import jax
import jax.numpy as jnp
from jax import lax
from jax.experimental import pallas as pl
from jax.experimental.pallas import tpu as pltpu
from jax.sharding import PartitionSpec as P

HD = 128
MESH = pl.DeviceIdType.MESH
NX = 4
NZ = 8
NF = NX * NZ
NY = 4
HL = 3
HC = 2 * HL
TOK = 1024
HALF = TOK // 2
ROWS = HALF // NF
PART = ROWS // 2
CH = TOK // NF
WL = HL * HD
WC = HC * HD
QB = 256
PB = 128
NP = PB // ROWS
SIZES = ((4, 4), (4, 5), (5, 4), (5, 5), (HC, HC))
GAIN = HD ** -0.5 * 1.4426950408889634


def rdma(src, dst, send_sem, recv_sem, where):
    return pltpu.make_async_remote_copy(
        src_ref=src, dst_ref=dst, send_sem=send_sem, recv_sem=recv_sem,
        device_id=where, device_id_type=MESH,
    )


def dot_t(a, b):
    return lax.dot_general(a, b, (((1,), (1,)), ((), ())), preferred_element_type=jnp.float32)


def dot(a, b):
    return jnp.dot(a, b, preferred_element_type=jnp.float32)


def kernel(
    slots, frees, kinds, qkv_in, weight, out,
    qkv6, kv_other, stage, recv, ostage, oret, kvst, kv0, kv1, sel, satt, att6, att, wfull,
    far_out, far_in, near_out, near_in, swap_out, swap_in, mine,
    loc_sem, px_send, px_recv, a_send, a_recv, o_send, o_recv,
    sc_send, sc_recv, zu_send, zd_send, z_recv, x_send, x_recv, y_send, y_recv,
):
    me = lax.axis_index("frame")
    mh = lax.axis_index("head")
    z, x = me // NX, me % NX
    y, c = mh // 2, mh % 2
    other = 1 - c
    partner = {"head": y * 2 + other}
    plus = {"head": lax.rem(y + 1, NY) * 2 + c}
    minus = {"head": lax.rem(y + NY - 1, NY) * 2 + c}

    barrier = pltpu.get_barrier_semaphore()

    def greet(j, carry):
        pl.semaphore_signal(
            barrier, inc=1, device_id={"frame": lax.rem(me + j, NF)}, device_id_type=MESH
        )
        return carry

    lax.fori_loop(1, NF, greet, 0)
    for who in (partner, plus, minus):
        pl.semaphore_signal(barrier, inc=1, device_id=who, device_id_type=MESH)

    my_rows = pl.ds(pl.multiple_of(c * HALF, HALF), HALF)
    other_rows = pl.ds(pl.multiple_of(other * HALF, HALF), HALF)
    my_lanes = pl.ds(pl.multiple_of(c * WL, HD), WL)
    other_lanes = pl.ds(pl.multiple_of(other * WL, HD), WL)
    my_wrows = pl.ds(pl.multiple_of(c * WL, HD), WL)

    own_qkv = pltpu.make_async_copy(
        qkv_in.at[:, my_rows, :], qkv6.at[:, :, my_lanes], loc_sem.at[0]
    )
    own_qkv.start()
    own_w = pltpu.make_async_copy(weight, wfull.at[my_wrows, :], loc_sem.at[1])
    own_w.start()

    own_kv = pltpu.make_async_copy(
        qkv_in.at[pl.ds(1, 2), other_rows, :], kv_other.at[:, :, my_lanes], loc_sem.at[2]
    )
    own_kv.start()

    pl.semaphore_wait(barrier, NF - 1 + 3)

    swap = rdma(
        qkv_in.at[:, other_rows, :], qkv6.at[:, :, my_lanes], px_send.at[0], px_recv.at[0], partner
    )
    swap.start()

    own_qkv.wait()
    rdma(
        qkv_in.at[:, my_rows, :], qkv6.at[:, :, other_lanes], px_send.at[0], px_recv.at[0], partner
    ).wait_recv()

    kind = [kinds[y * HC + h] for h in range(HC)]
    place = [0]
    for h in range(HC - 1):
        place.append(place[-1] + kind[h])
    free = [h - place[h] for h in range(HC)]

    def chosen(ref, i, rows, wanted, place_of, slot, low):
        part = ref[i, rows, low * HD : (low + 1) * HD]
        for h in range(low + 1, HC):
            here = (kind[h] == wanted) & (place_of[h] == slot)
            part = jnp.where(here, ref[i, rows, h * HD : (h + 1) * HD], part)
        return part

    def in_pieces(body):
        def step(b, carry):
            body(b, pl.ds(pl.multiple_of(b * PB, PB), PB))
            return carry

        lax.fori_loop(0, HALF // PB, step, 0)

    @pl.when(me == 0)
    def _():
        def fill_first(b, rows):
            for n in range(frees):
                for i in range(2):
                    part = chosen(qkv6, 1 + i, rows, 0, free, n, n)
                    kvst[pl.ds(b * NP, NP), n, i] = part.reshape(NP, ROWS, HD)

        in_pieces(fill_first)
        pltpu.make_async_copy(kvst.at[0], kv0.at[0, 0], sc_recv).start()

        def scatter(j, carry):
            rdma(
                kvst.at[j], kv0.at[j // NX, j % NX], sc_send.at[j], sc_recv, {"frame": j}
            ).start()
            return carry

        lax.fori_loop(1, NF, scatter, 0)

    def fill_stage(b, rows):
        for t in range(slots):
            for i in range(3):
                part = chosen(qkv6, i, rows, 1, place, t, t)
                stage[pl.ds(b * NP, NP), t, i] = part.reshape(NP, ROWS, HD)

    in_pieces(fill_stage)

    def send_part(dz, dx):
        to = lax.rem(z + dz, NZ) * NX + lax.rem(x + dx, NX)
        rdma(stage.at[to], recv.at[me], a_send.at[to], a_recv.at[me], {"frame": to}).start()

    def turn(n):
        odd = lax.rem(n, 2)
        return odd * ((n + 1) // 2) + (1 - odd) * (NZ - n // 2)

    def send_straight(n, carry):
        send_part(turn(n), 0)
        return carry

    def send_row(n, carry):
        send_part(0, n)
        return carry

    def send_rest(n, carry):
        send_part(turn(n // (NX - 1) + 1), n % (NX - 1) + 1)
        return carry

    pltpu.make_async_copy(kvst.at[0], kv0.at[z, x], sc_recv).wait()

    z_up = {"frame": lax.rem(z + 1, NZ) * NX + x}
    z_down = {"frame": lax.rem(z + NZ - 1, NZ) * NX + x}
    x_up = {"frame": z * NX + lax.rem(x + 1, NX)}
    x_down = {"frame": z * NX + lax.rem(x + NX - 1, NX)}
    ring = []

    def pass_on(src, send_sem, recv_sem, who):
        copy = rdma(src, src, send_sem, recv_sem, who)
        copy.start()
        ring.append(copy)

    def arrived(part, recv_sem):
        rdma(part, part, zu_send.at[0], recv_sem, z_up).wait_recv()

    for step in range(NZ // 2):
        low = lax.rem(z + NZ - step, NZ)
        high = lax.rem(z + step, NZ)
        if step > 0:
            arrived(kv0.at[low, x], z_recv.at[low])
        pass_on(kv0.at[low, x], zu_send.at[step], z_recv.at[low], z_up)
        if step < NZ // 2 - 1:
            if step > 0:
                arrived(kv0.at[high, x], z_recv.at[high])
            pass_on(kv0.at[high, x], zd_send.at[step], z_recv.at[high], z_down)
    for at in (lax.rem(z + NZ // 2, NZ), lax.rem(z + NZ // 2 - 1, NZ)):
        arrived(kv0.at[at, x], z_recv.at[at])
    x_low, x_high = lax.rem(x + NX - 1, NX), lax.rem(x + 1, NX)
    x_over = lax.rem(x + 2, NX)
    pass_on(kv0.at[:, x], x_send.at[0], x_recv.at[x], x_up)
    pass_on(kv0.at[:, x], x_send.at[1], x_recv.at[x], x_down)

    lax.fori_loop(1, NZ, send_straight, 0)

    near_z, far_z = pl.ds(0, NZ // 2), pl.ds(NZ // 2, NZ // 2)
    arrived(kv0.at[:, x_low], x_recv.at[x_low])
    pass_on(kv0.at[near_z, x_low], x_send.at[2], x_recv.at[NX], x_up)
    arrived(kv0.at[:, x_high], x_recv.at[x_high])
    pass_on(kv0.at[far_z, x_high], x_send.at[3], x_recv.at[NX + 1], x_down)
    arrived(kv0.at[near_z, x_over], x_recv.at[NX])
    arrived(kv0.at[far_z, x_over], x_recv.at[NX + 1])
    share_first = rdma(kv0, kv1, px_send.at[2], px_recv.at[2], partner)
    share_first.start()
    share_kv = rdma(
        qkv_in.at[pl.ds(1, 2), my_rows, :], kv_other.at[:, :, my_lanes],
        px_send.at[5], px_recv.at[5], partner,
    )
    share_kv.start()
    lax.fori_loop(1, NX, send_row, 0)
    lax.fori_loop(0, (NZ - 1) * (NX - 1), send_rest, 0)
    recv[pl.ds(me, 1)] = stage[pl.ds(me, 1)]

    swap_w = rdma(weight, wfull.at[my_wrows, :], px_send.at[1], px_recv.at[1], partner)
    swap_w.start()


    own_kv.wait()
    share_first.wait_recv()
    rdma(
        qkv_in.at[pl.ds(1, 2), my_rows, :], kv_other.at[:, :, other_lanes],
        px_send.at[5], px_recv.at[5], partner,
    ).wait_recv()

    def spatial(n, carry):
        def select(b, rows):
            for at, (ref, i) in enumerate(
                ((qkv6, 0), (qkv6, 1), (kv_other, 0), (qkv6, 2), (kv_other, 1))
            ):
                sel[at, rows, :] = chosen(ref, i, rows, 0, free, n, 0)

        in_pieces(select)

        def block(b, inner):
            rows = pl.ds(pl.multiple_of(b * QB, QB), QB)
            q = sel[0, rows, :]
            firsts = [ref[:, :, n, 0].reshape(HALF, HD) for ref in (kv0, kv1)]
            scores = [dot_t(q, sel[1]), dot_t(q, sel[2])]
            scores += [jnp.where(me == 0, -1e30, dot_t(q, keys)) for keys in firsts]
            top = functools.reduce(
                jnp.maximum, [jnp.max(s, axis=-1, keepdims=True) for s in scores]
            )
            values = [sel[3], sel[4]] + [ref[:, :, n, 1].reshape(HALF, HD) for ref in (kv0, kv1)]
            norm, mixed = 0.0, 0.0
            for s, v in zip(scores, values):
                e = jnp.exp2((s - top) * GAIN)
                norm += jnp.sum(e, axis=-1, keepdims=True)
                mixed += dot(e.astype(jnp.bfloat16), v)
            satt[n, rows, :] = (mixed / norm).astype(jnp.bfloat16)
            return inner

        return lax.fori_loop(0, HALF // QB, block, carry)

    lax.fori_loop(0, frees, spatial, 0)

    def rows_of(tile, k):
        wide = tile.astype(jnp.float32)
        return wide[:, k * PART : (k + 1) * PART].reshape(-1, HD)

    def order(b, rows):
        for h in range(HC):
            part = satt[0, rows, :]
            for n in range(1, min(h + 1, frees)):
                part = jnp.where(free[h] == n, satt[n, rows, :], part)
            for k in range(2):
                att6[k, pl.ds(pl.multiple_of(b * PB // 2, PB // 2), PB // 2), h * HD : (h + 1) * HD] = (
                    rows_of(part.reshape(NP, ROWS, HD), k).astype(jnp.bfloat16)
                )

    in_pieces(order)
    own_w.wait()
    rdma(
        weight, wfull.at[pl.ds(pl.multiple_of(other * WL, HD), WL), :],
        px_send.at[1], px_recv.at[1], partner,
    ).wait_recv()

    def wait_parts(j, carry):
        at = lax.rem(me + NF - j, NF)
        rdma(stage.at[at], recv.at[at], a_send.at[at], a_recv.at[at], {"frame": at}).wait_recv()
        return carry

    lax.fori_loop(1, NF, wait_parts, 0)

    span = NF * PART
    same = (
        lax.broadcasted_iota(jnp.int32, (span, span), 0) % PART
        == lax.broadcasted_iota(jnp.int32, (span, span), 1) % PART
    )

    def temporal(t, k):
        q, key, v = (rows_of(recv[:, t, i], k).astype(jnp.bfloat16) for i in range(3))
        s = jnp.where(same, dot_t(q, key), -1e30)
        e = jnp.exp2((s - jnp.max(s, axis=-1, keepdims=True)) * GAIN)
        norm = jnp.sum(e, axis=-1, keepdims=True)
        return (dot(e.astype(jnp.bfloat16), v) / norm).reshape(NF, PART, HD)

    def back(to, k):
        return rdma(
            ostage.at[to, k], oret.at[me, k], o_send.at[k, to], o_recv.at[k, me], {"frame": to}
        )

    for k in range(2):

        def pair(n, carry, k=k):
            both = [temporal(jnp.minimum(2 * n + i, slots - 1), k) for i in range(2)]
            ostage[:, k, n] = jnp.concatenate(both, axis=1).astype(jnp.bfloat16)
            return carry

        lax.fori_loop(0, (slots + 1) // 2, pair, 0)

        def send_back(j, carry, k=k):
            back(lax.rem(me + j, NF), k).start()
            return carry

        lax.fori_loop(1, NF, send_back, 0)
        oret[pl.ds(me, 1), k] = ostage[pl.ds(me, 1), k]

    def product(dst, k, block, half, *more):
        lanes = pl.ds(pl.multiple_of(block * WC + half * WL, HD), WL)

        def piece(b, carry):
            rows = pl.ds(pl.multiple_of(b * PB, PB), PB)
            total = dot(att[k, rows, :], wfull[:, lanes])
            for extra in more:
                total += extra[rows, :].astype(jnp.float32)
            dst[rows, :] = total.astype(jnp.bfloat16)
            return carry

        lax.fori_loop(0, span // PB, piece, 0)

    up, down, far = lax.rem(y + 1, NY), lax.rem(y + NY - 1, NY), lax.rem(y + 2, NY)

    def y_copy(k, index):
        parts = (
            (far_out.at[k, 0], far_in.at[k, 0], plus),
            (far_out.at[k, 1], far_in.at[k, 1], minus),
            (near_out.at[k, 0, 1], near_in.at[k, 0, 1], plus),
            (near_out.at[k, 1, 0], near_in.at[k, 1, 0], minus),
            (near_out.at[k, 0, 0], near_in.at[k, 0, 0], plus),
            (near_out.at[k, 1, 1], near_in.at[k, 1, 1], minus),
        )
        src, dst, who = parts[index]
        return rdma(src, dst, y_send.at[k, index], y_recv.at[k, index], who)

    def reduce_chunk(k, carry):
        def wait_back(j, inner):
            at = lax.rem(me + NF - j, NF)
            rdma(
                ostage.at[at, k], oret.at[at, k], o_send.at[k, at], o_recv.at[k, at],
                {"frame": at},
            ).wait_recv()
            return inner

        lax.fori_loop(1, NF, wait_back, 0)

        def gather(b, rows):
            half_rows = pl.ds(pl.multiple_of(b * PB // 2, PB // 2), PB // 2)
            for h in range(HC):
                lanes = slice(h * HD, (h + 1) * HD)
                part = att6[k, half_rows, lanes].astype(jnp.float32)
                for t in range(min(h + 1, slots)):
                    here = (kind[h] == 1) & (place[h] == t)
                    returned = rows_of(oret[pl.ds(b * NP, NP), k, t // 2], t % 2)
                    part = jnp.where(here, returned, part)
                att[k, half_rows, lanes] = part.astype(jnp.bfloat16)

        in_pieces(gather)

        product(far_out.at[k, 0], k, far, 0)
        y_copy(k, 0).start()
        product(far_out.at[k, 1], k, far, 1)
        y_copy(k, 1).start()
        product(near_out.at[k, 0, 1], k, up, 1)
        y_copy(k, 2).start()
        product(near_out.at[k, 1, 0], k, down, 0)
        y_copy(k, 3).start()
        y_copy(k, 0).wait_recv()
        product(near_out.at[k, 0, 0], k, up, 0, far_in.at[k, 0])
        y_copy(k, 4).start()
        y_copy(k, 1).wait_recv()
        product(near_out.at[k, 1, 1], k, down, 1, far_in.at[k, 1])
        y_copy(k, 5).start()
        return carry

    lax.fori_loop(0, 2, reduce_chunk, 0)

    def swap_copy(k):
        return rdma(
            swap_out.at[k], swap_in.at[k], px_send.at[3 + k], px_recv.at[3 + k], partner
        )

    def finish(k, carry):
        for index in range(2, 6):
            y_copy(k, index).wait_recv()
        product(swap_out.at[k], k, y, other, near_in.at[k, 0, other], near_in.at[k, 1, other])
        swap_copy(k).start()
        product(mine.at[k], k, y, c, near_in.at[k, 0, c], near_in.at[k, 1, c])
        return carry

    lax.fori_loop(0, 2, finish, 0)

    def join(src):
        tiles = [src[k].astype(jnp.float32).reshape(NF, PART, WL) for k in range(2)]
        return jnp.concatenate(tiles, axis=1).reshape(HALF, WL).astype(jnp.bfloat16)

    out[my_rows, :] = join(mine)
    for k in range(2):
        swap_copy(k).wait_recv()
    out[other_rows, :] = join(swap_in)

    swap.wait_send()
    swap_w.wait_send()
    share_first.wait_send()
    share_kv.wait_send()
    for k in range(2):
        swap_copy(k).wait_send()
        for index in range(6):
            y_copy(k, index).wait_send()

    def drain(j, carry):
        to = lax.rem(me + j, NF)
        rdma(stage.at[to], recv.at[me], a_send.at[to], a_recv.at[me], {"frame": to}).wait_send()
        back(to, 0).wait_send()
        back(to, 1).wait_send()
        return carry

    lax.fori_loop(1, NF, drain, 0)

    for copy in ring:
        copy.wait_send()

    @pl.when(me == 0)
    def _():
        def drain_s(j, carry):
            rdma(
                kvst.at[j], kv0.at[j // NX, j % NX], sc_send.at[j], sc_recv, {"frame": j}
            ).wait_send()
            return carry

        lax.fori_loop(1, NF, drain_s, 0)


def attention(slots, frees, ident, kinds, qkv, weight):
    bf = jnp.bfloat16
    vmem = pl.BlockSpec(memory_space=pltpu.VMEM)
    hbm = pl.BlockSpec(memory_space=pl.ANY)
    dma = pltpu.SemaphoreType.DMA
    return pl.pallas_call(
        functools.partial(kernel, slots, frees),
        out_shape=jax.ShapeDtypeStruct((TOK, WL), bf),
        in_specs=[pl.BlockSpec(memory_space=pltpu.SMEM), hbm, hbm],
        out_specs=vmem,
        scratch_shapes=[
            pltpu.VMEM((3, HALF, WC), bf),
            pltpu.VMEM((2, HALF, WC), bf),
            pltpu.VMEM((NF, slots, 3, ROWS, HD), bf),
            pltpu.VMEM((NF, slots, 3, ROWS, HD), bf),
            pltpu.VMEM((NF, 2, (slots + 1) // 2, ROWS, HD), bf),
            pltpu.VMEM((NF, 2, (slots + 1) // 2, ROWS, HD), bf),
            pltpu.VMEM((NF, frees, 2, ROWS, HD), bf),
            pltpu.VMEM((NZ, NX, frees, 2, ROWS, HD), bf),
            pltpu.VMEM((NZ, NX, frees, 2, ROWS, HD), bf),
            pltpu.VMEM((5, HALF, HD), bf),
            pltpu.VMEM((frees, HALF, HD), bf),
            pltpu.VMEM((2, HALF // 2, WC), bf),
            pltpu.VMEM((2, HALF // 2, WC), bf),
            pltpu.VMEM((WC, NY * WC), bf),
            pltpu.VMEM((2, 2, HALF // 2, WL), bf),
            pltpu.VMEM((2, 2, HALF // 2, WL), bf),
            pltpu.VMEM((2, 2, 2, HALF // 2, WL), bf),
            pltpu.VMEM((2, 2, 2, HALF // 2, WL), bf),
            pltpu.VMEM((2, HALF // 2, WL), bf),
            pltpu.VMEM((2, HALF // 2, WL), bf),
            pltpu.VMEM((2, HALF // 2, WL), bf),
            dma((4,)),
            dma((6,)), dma((6,)),
            dma((NF,)), dma((NF,)),
            dma((2, NF)), dma((2, NF)),
            dma((NF,)), dma,
            dma((NZ,)), dma((NZ,)), dma((NZ,)),
            dma((NX,)), dma((NX + 2,)),
            dma((2, 6)), dma((2, 6)),
        ],
        compiler_params=pltpu.CompilerParams(
            collective_id=ident, has_side_effects=True, vmem_limit_bytes=56 * 1024 * 1024
        ),
    )(kinds, qkv, weight)


def local(qkv, head_kinds, out_weight):
    chip = jnp.arange(NY * HC) // HC == jnp.arange(NY)[:, None]
    counts = jnp.sum(jnp.where(chip, head_kinds, 0), axis=1)
    more = jnp.maximum(counts - SIZES[0][0], 0)[:, None]
    fewer = jnp.maximum(HC - SIZES[0][1] - counts, 0)[None, :]
    index = jnp.max(jnp.where((more > 1) | (fewer > 1), len(SIZES) - 1, 2 * more + fewer))
    choices = [
        functools.partial(attention, slots, frees, ident)
        for ident, (slots, frees) in enumerate(SIZES)
    ]
    return lax.switch(index, choices, head_kinds, qkv.transpose(1, 0, 2), out_weight)


def solution(mesh):
    placed = (P("frame", None, "head"), P(), P("head", None))
    return jax.shard_map(
        local, mesh=mesh, in_specs=placed, out_specs=P("frame", "head"), check_vma=False
    )
```

```python
import functools

import jax
import jax.numpy as jnp
from jax import lax
from jax.experimental import pallas as pl
from jax.experimental.pallas import tpu as pltpu
from jax.sharding import PartitionSpec as P

HD = 128
MESH = pl.DeviceIdType.MESH
NX = 4
NZ = 8
NF = NX * NZ
NY = 4
HL = 3
HC = 2 * HL
TOK = 1024
HALF = TOK // 2
ROWS = HALF // NF
PART = ROWS // 2
CH = TOK // NF
WL = HL * HD
WC = HC * HD
QB = 256
PB = 256
NP = PB // ROWS
SIZES = ((4, 4), (4, 5), (5, 4), (5, 5), (HC, HC))
GAIN = HD ** -0.5 * 1.4426950408889634


def rdma(src, dst, send_sem, recv_sem, where):
    return pltpu.make_async_remote_copy(
        src_ref=src, dst_ref=dst, send_sem=send_sem, recv_sem=recv_sem,
        device_id=where, device_id_type=MESH,
    )


def dot_t(a, b):
    return lax.dot_general(a, b, (((1,), (1,)), ((), ())), preferred_element_type=jnp.float32)


def dot(a, b):
    return jnp.dot(a, b, preferred_element_type=jnp.float32)


def kernel(
    slots, frees, kinds, qkv_in, weight, out,
    qkv6, kv_other, stage, recv, ostage, oret, kvst, kv0, kv1, sel, satt, att6, att, wfull,
    far_out, far_in, near_out, near_in, swap_out, swap_in, mine,
    loc_sem, px_send, px_recv, a_send, a_recv, o_send, o_recv,
    sc_send, sc_recv, zu_send, zd_send, z_recv, x_send, x_recv, y_send, y_recv,
):
    me = lax.axis_index("frame")
    mh = lax.axis_index("head")
    z, x = me // NX, me % NX
    y, c = mh // 2, mh % 2
    other = 1 - c
    partner = {"head": y * 2 + other}
    plus = {"head": lax.rem(y + 1, NY) * 2 + c}
    minus = {"head": lax.rem(y + NY - 1, NY) * 2 + c}

    barrier = pltpu.get_barrier_semaphore()

    def greet(j, carry):
        pl.semaphore_signal(
            barrier, inc=1, device_id={"frame": lax.rem(me + j, NF)}, device_id_type=MESH
        )
        return carry

    lax.fori_loop(1, NF, greet, 0)
    for who in (partner, plus, minus):
        pl.semaphore_signal(barrier, inc=1, device_id=who, device_id_type=MESH)

    my_rows = pl.ds(pl.multiple_of(c * HALF, HALF), HALF)
    other_rows = pl.ds(pl.multiple_of(other * HALF, HALF), HALF)
    my_lanes = pl.ds(pl.multiple_of(c * WL, HD), WL)
    other_lanes = pl.ds(pl.multiple_of(other * WL, HD), WL)
    my_wrows = pl.ds(pl.multiple_of(c * WL, HD), WL)

    own_qkv = pltpu.make_async_copy(
        qkv_in.at[:, my_rows, :], qkv6.at[:, :, my_lanes], loc_sem.at[0]
    )
    own_qkv.start()
    own_w = pltpu.make_async_copy(weight, wfull.at[my_wrows, :], loc_sem.at[1])
    own_w.start()

    own_kv = pltpu.make_async_copy(
        qkv_in.at[pl.ds(1, 2), other_rows, :], kv_other.at[:, :, my_lanes], loc_sem.at[2]
    )
    own_kv.start()

    pl.semaphore_wait(barrier, NF - 1 + 3)

    swap = rdma(
        qkv_in.at[:, other_rows, :], qkv6.at[:, :, my_lanes], px_send.at[0], px_recv.at[0], partner
    )
    swap.start()

    own_qkv.wait()
    rdma(
        qkv_in.at[:, my_rows, :], qkv6.at[:, :, other_lanes], px_send.at[0], px_recv.at[0], partner
    ).wait_recv()

    kind = [kinds[y * HC + h] for h in range(HC)]
    place = [0]
    for h in range(HC - 1):
        place.append(place[-1] + kind[h])
    free = [h - place[h] for h in range(HC)]

    def chosen(ref, i, rows, wanted, place_of, slot, low):
        part = ref[i, rows, low * HD : (low + 1) * HD]
        for h in range(low + 1, HC):
            here = (kind[h] == wanted) & (place_of[h] == slot)
            part = jnp.where(here, ref[i, rows, h * HD : (h + 1) * HD], part)
        return part

    def in_pieces(body):
        def step(b, carry):
            body(b, pl.ds(pl.multiple_of(b * PB, PB), PB))
            return carry

        lax.fori_loop(0, HALF // PB, step, 0)

    @pl.when(me == 0)
    def _():
        def fill_first(b, rows):
            for n in range(frees):
                for i in range(2):
                    part = chosen(qkv6, 1 + i, rows, 0, free, n, n)
                    kvst[pl.ds(b * NP, NP), n, i] = part.reshape(NP, ROWS, HD)

        in_pieces(fill_first)
        pltpu.make_async_copy(kvst.at[0], kv0.at[0, 0], sc_recv).start()

        def scatter(j, carry):
            rdma(
                kvst.at[j], kv0.at[j // NX, j % NX], sc_send.at[j], sc_recv, {"frame": j}
            ).start()
            return carry

        lax.fori_loop(1, NF, scatter, 0)

    def fill_stage(b, rows):
        for t in range(slots):
            for i in range(3):
                part = chosen(qkv6, i, rows, 1, place, t, t)
                stage[pl.ds(b * NP, NP), t, i] = part.reshape(NP, ROWS, HD)

    in_pieces(fill_stage)

    def send_part(dz, dx):
        to = lax.rem(z + dz, NZ) * NX + lax.rem(x + dx, NX)
        rdma(stage.at[to], recv.at[me], a_send.at[to], a_recv.at[me], {"frame": to}).start()

    def turn(n):
        odd = lax.rem(n, 2)
        return odd * ((n + 1) // 2) + (1 - odd) * (NZ - n // 2)

    def send_straight(n, carry):
        send_part(turn(n), 0)
        return carry

    def send_row(n, carry):
        send_part(0, n)
        return carry

    def send_rest(n, carry):
        send_part(turn(n // (NX - 1) + 1), n % (NX - 1) + 1)
        return carry

    pltpu.make_async_copy(kvst.at[0], kv0.at[z, x], sc_recv).wait()

    z_up = {"frame": lax.rem(z + 1, NZ) * NX + x}
    z_down = {"frame": lax.rem(z + NZ - 1, NZ) * NX + x}
    x_up = {"frame": z * NX + lax.rem(x + 1, NX)}
    x_down = {"frame": z * NX + lax.rem(x + NX - 1, NX)}
    ring = []

    def pass_on(src, send_sem, recv_sem, who):
        copy = rdma(src, src, send_sem, recv_sem, who)
        copy.start()
        ring.append(copy)

    def arrived(part, recv_sem):
        rdma(part, part, zu_send.at[0], recv_sem, z_up).wait_recv()

    for step in range(NZ // 2):
        low = lax.rem(z + NZ - step, NZ)
        high = lax.rem(z + step, NZ)
        if step > 0:
            arrived(kv0.at[low, x], z_recv.at[low])
        pass_on(kv0.at[low, x], zu_send.at[step], z_recv.at[low], z_up)
        if step < NZ // 2 - 1:
            if step > 0:
                arrived(kv0.at[high, x], z_recv.at[high])
            pass_on(kv0.at[high, x], zd_send.at[step], z_recv.at[high], z_down)
    for at in (lax.rem(z + NZ // 2, NZ), lax.rem(z + NZ // 2 - 1, NZ)):
        arrived(kv0.at[at, x], z_recv.at[at])
    x_low, x_high = lax.rem(x + NX - 1, NX), lax.rem(x + 1, NX)
    x_over = lax.rem(x + 2, NX)
    pass_on(kv0.at[:, x], x_send.at[0], x_recv.at[x], x_up)
    pass_on(kv0.at[:, x], x_send.at[1], x_recv.at[x], x_down)

    lax.fori_loop(1, NZ, send_straight, 0)

    near_z, far_z = pl.ds(0, NZ // 2), pl.ds(NZ // 2, NZ // 2)
    arrived(kv0.at[:, x_low], x_recv.at[x_low])
    pass_on(kv0.at[near_z, x_low], x_send.at[2], x_recv.at[NX], x_up)
    arrived(kv0.at[:, x_high], x_recv.at[x_high])
    pass_on(kv0.at[far_z, x_high], x_send.at[3], x_recv.at[NX + 1], x_down)
    arrived(kv0.at[near_z, x_over], x_recv.at[NX])
    arrived(kv0.at[far_z, x_over], x_recv.at[NX + 1])
    share_first = rdma(kv0, kv1, px_send.at[2], px_recv.at[2], partner)
    share_first.start()
    share_kv = rdma(
        qkv_in.at[pl.ds(1, 2), my_rows, :], kv_other.at[:, :, my_lanes],
        px_send.at[5], px_recv.at[5], partner,
    )
    share_kv.start()
    lax.fori_loop(1, NX, send_row, 0)
    lax.fori_loop(0, (NZ - 1) * (NX - 1), send_rest, 0)
    recv[pl.ds(me, 1)] = stage[pl.ds(me, 1)]

    swap_w = rdma(weight, wfull.at[my_wrows, :], px_send.at[1], px_recv.at[1], partner)
    swap_w.start()


    own_kv.wait()
    share_first.wait_recv()
    rdma(
        qkv_in.at[pl.ds(1, 2), my_rows, :], kv_other.at[:, :, other_lanes],
        px_send.at[5], px_recv.at[5], partner,
    ).wait_recv()

    def spatial(n, carry):
        def select(b, rows):
            for at, (ref, i) in enumerate(
                ((qkv6, 0), (qkv6, 1), (kv_other, 0), (qkv6, 2), (kv_other, 1))
            ):
                sel[at, rows, :] = chosen(ref, i, rows, 0, free, n, 0)

        in_pieces(select)

        def block(b, inner):
            rows = pl.ds(pl.multiple_of(b * QB, QB), QB)
            q = sel[0, rows, :]
            firsts = [ref[:, :, n, 0].reshape(HALF, HD) for ref in (kv0, kv1)]
            scores = [dot_t(q, sel[1]), dot_t(q, sel[2])]
            scores += [jnp.where(me == 0, -1e30, dot_t(q, keys)) for keys in firsts]
            top = functools.reduce(
                jnp.maximum, [jnp.max(s, axis=-1, keepdims=True) for s in scores]
            )
            values = [sel[3], sel[4]] + [ref[:, :, n, 1].reshape(HALF, HD) for ref in (kv0, kv1)]
            norm, mixed = 0.0, 0.0
            for s, v in zip(scores, values):
                e = jnp.exp2((s - top) * GAIN)
                norm += jnp.sum(e, axis=-1, keepdims=True)
                mixed += dot(e.astype(jnp.bfloat16), v)
            satt[n, rows, :] = (mixed / norm).astype(jnp.bfloat16)
            return inner

        return lax.fori_loop(0, HALF // QB, block, carry)

    lax.fori_loop(0, frees, spatial, 0)

    def rows_of(tile, k):
        wide = tile.astype(jnp.float32)
        return wide[:, k * PART : (k + 1) * PART].reshape(-1, HD)

    def order(b, rows):
        for h in range(HC):
            part = satt[0, rows, :]
            for n in range(1, min(h + 1, frees)):
                part = jnp.where(free[h] == n, satt[n, rows, :], part)
            for k in range(2):
                att6[k, pl.ds(pl.multiple_of(b * PB // 2, PB // 2), PB // 2), h * HD : (h + 1) * HD] = (
                    rows_of(part.reshape(NP, ROWS, HD), k).astype(jnp.bfloat16)
                )

    in_pieces(order)
    own_w.wait()
    rdma(
        weight, wfull.at[pl.ds(pl.multiple_of(other * WL, HD), WL), :],
        px_send.at[1], px_recv.at[1], partner,
    ).wait_recv()

    def wait_parts(j, carry):
        at = lax.rem(me + NF - j, NF)
        rdma(stage.at[at], recv.at[at], a_send.at[at], a_recv.at[at], {"frame": at}).wait_recv()
        return carry

    lax.fori_loop(1, NF, wait_parts, 0)

    span = NF * PART
    same = (
        lax.broadcasted_iota(jnp.int32, (span, span), 0) % PART
        == lax.broadcasted_iota(jnp.int32, (span, span), 1) % PART
    )

    def temporal(t, k):
        q, key, v = (rows_of(recv[:, t, i], k).astype(jnp.bfloat16) for i in range(3))
        s = jnp.where(same, dot_t(q, key), -1e30)
        e = jnp.exp2((s - jnp.max(s, axis=-1, keepdims=True)) * GAIN)
        norm = jnp.sum(e, axis=-1, keepdims=True)
        return (dot(e.astype(jnp.bfloat16), v) / norm).reshape(NF, PART, HD)

    def back(to, k):
        return rdma(
            ostage.at[to, k], oret.at[me, k], o_send.at[k, to], o_recv.at[k, me], {"frame": to}
        )

    for k in range(2):

        def pair(n, carry, k=k):
            both = [temporal(jnp.minimum(2 * n + i, slots - 1), k) for i in range(2)]
            ostage[:, k, n] = jnp.concatenate(both, axis=1).astype(jnp.bfloat16)
            return carry

        lax.fori_loop(0, (slots + 1) // 2, pair, 0)

        def send_back(j, carry, k=k):
            back(lax.rem(me + j, NF), k).start()
            return carry

        lax.fori_loop(1, NF, send_back, 0)
        oret[pl.ds(me, 1), k] = ostage[pl.ds(me, 1), k]

    def product(dst, k, block, half, *more):
        lanes = pl.ds(pl.multiple_of(block * WC + half * WL, HD), WL)

        def piece(b, carry):
            rows = pl.ds(pl.multiple_of(b * PB, PB), PB)
            total = dot(att[k, rows, :], wfull[:, lanes])
            for extra in more:
                total += extra[rows, :].astype(jnp.float32)
            dst[rows, :] = total.astype(jnp.bfloat16)
            return carry

        lax.fori_loop(0, span // PB, piece, 0)

    up, down, far = lax.rem(y + 1, NY), lax.rem(y + NY - 1, NY), lax.rem(y + 2, NY)

    def y_copy(k, index):
        parts = (
            (far_out.at[k, 0], far_in.at[k, 0], plus),
            (far_out.at[k, 1], far_in.at[k, 1], minus),
            (near_out.at[k, 0, 1], near_in.at[k, 0, 1], plus),
            (near_out.at[k, 1, 0], near_in.at[k, 1, 0], minus),
            (near_out.at[k, 0, 0], near_in.at[k, 0, 0], plus),
            (near_out.at[k, 1, 1], near_in.at[k, 1, 1], minus),
        )
        src, dst, who = parts[index]
        return rdma(src, dst, y_send.at[k, index], y_recv.at[k, index], who)

    def reduce_chunk(k, carry):
        def wait_back(j, inner):
            at = lax.rem(me + NF - j, NF)
            rdma(
                ostage.at[at, k], oret.at[at, k], o_send.at[k, at], o_recv.at[k, at],
                {"frame": at},
            ).wait_recv()
            return inner

        lax.fori_loop(1, NF, wait_back, 0)

        def gather(b, rows):
            half_rows = pl.ds(pl.multiple_of(b * PB // 2, PB // 2), PB // 2)
            for h in range(HC):
                lanes = slice(h * HD, (h + 1) * HD)
                part = att6[k, half_rows, lanes].astype(jnp.float32)
                for t in range(min(h + 1, slots)):
                    here = (kind[h] == 1) & (place[h] == t)
                    returned = rows_of(oret[pl.ds(b * NP, NP), k, t // 2], t % 2)
                    part = jnp.where(here, returned, part)
                att[k, half_rows, lanes] = part.astype(jnp.bfloat16)

        in_pieces(gather)

        product(far_out.at[k, 0], k, far, 0)
        y_copy(k, 0).start()
        product(far_out.at[k, 1], k, far, 1)
        y_copy(k, 1).start()
        product(near_out.at[k, 0, 1], k, up, 1)
        y_copy(k, 2).start()
        product(near_out.at[k, 1, 0], k, down, 0)
        y_copy(k, 3).start()
        y_copy(k, 0).wait_recv()
        product(near_out.at[k, 0, 0], k, up, 0, far_in.at[k, 0])
        y_copy(k, 4).start()
        y_copy(k, 1).wait_recv()
        product(near_out.at[k, 1, 1], k, down, 1, far_in.at[k, 1])
        y_copy(k, 5).start()
        return carry

    lax.fori_loop(0, 2, reduce_chunk, 0)

    def swap_copy(k):
        return rdma(
            swap_out.at[k], swap_in.at[k], px_send.at[3 + k], px_recv.at[3 + k], partner
        )

    def finish(k, carry):
        for index in range(2, 6):
            y_copy(k, index).wait_recv()
        product(swap_out.at[k], k, y, other, near_in.at[k, 0, other], near_in.at[k, 1, other])
        swap_copy(k).start()
        product(mine.at[k], k, y, c, near_in.at[k, 0, c], near_in.at[k, 1, c])
        return carry

    lax.fori_loop(0, 2, finish, 0)

    def join(src):
        tiles = [src[k].astype(jnp.float32).reshape(NF, PART, WL) for k in range(2)]
        return jnp.concatenate(tiles, axis=1).reshape(HALF, WL).astype(jnp.bfloat16)

    out[my_rows, :] = join(mine)
    for k in range(2):
        swap_copy(k).wait_recv()
    out[other_rows, :] = join(swap_in)

    swap.wait_send()
    swap_w.wait_send()
    share_first.wait_send()
    share_kv.wait_send()
    for k in range(2):
        swap_copy(k).wait_send()
        for index in range(6):
            y_copy(k, index).wait_send()

    def drain(j, carry):
        to = lax.rem(me + j, NF)
        rdma(stage.at[to], recv.at[me], a_send.at[to], a_recv.at[me], {"frame": to}).wait_send()
        back(to, 0).wait_send()
        back(to, 1).wait_send()
        return carry

    lax.fori_loop(1, NF, drain, 0)

    for copy in ring:
        copy.wait_send()

    @pl.when(me == 0)
    def _():
        def drain_s(j, carry):
            rdma(
                kvst.at[j], kv0.at[j // NX, j % NX], sc_send.at[j], sc_recv, {"frame": j}
            ).wait_send()
            return carry

        lax.fori_loop(1, NF, drain_s, 0)


def attention(slots, frees, ident, kinds, qkv, weight):
    bf = jnp.bfloat16
    vmem = pl.BlockSpec(memory_space=pltpu.VMEM)
    hbm = pl.BlockSpec(memory_space=pl.ANY)
    dma = pltpu.SemaphoreType.DMA
    return pl.pallas_call(
        functools.partial(kernel, slots, frees),
        out_shape=jax.ShapeDtypeStruct((TOK, WL), bf),
        in_specs=[pl.BlockSpec(memory_space=pltpu.SMEM), hbm, hbm],
        out_specs=vmem,
        scratch_shapes=[
            pltpu.VMEM((3, HALF, WC), bf),
            pltpu.VMEM((2, HALF, WC), bf),
            pltpu.VMEM((NF, slots, 3, ROWS, HD), bf),
            pltpu.VMEM((NF, slots, 3, ROWS, HD), bf),
            pltpu.VMEM((NF, 2, (slots + 1) // 2, ROWS, HD), bf),
            pltpu.VMEM((NF, 2, (slots + 1) // 2, ROWS, HD), bf),
            pltpu.VMEM((NF, frees, 2, ROWS, HD), bf),
            pltpu.VMEM((NZ, NX, frees, 2, ROWS, HD), bf),
            pltpu.VMEM((NZ, NX, frees, 2, ROWS, HD), bf),
            pltpu.VMEM((5, HALF, HD), bf),
            pltpu.VMEM((frees, HALF, HD), bf),
            pltpu.VMEM((2, HALF // 2, WC), bf),
            pltpu.VMEM((2, HALF // 2, WC), bf),
            pltpu.VMEM((WC, NY * WC), bf),
            pltpu.VMEM((2, 2, HALF // 2, WL), bf),
            pltpu.VMEM((2, 2, HALF // 2, WL), bf),
            pltpu.VMEM((2, 2, 2, HALF // 2, WL), bf),
            pltpu.VMEM((2, 2, 2, HALF // 2, WL), bf),
            pltpu.VMEM((2, HALF // 2, WL), bf),
            pltpu.VMEM((2, HALF // 2, WL), bf),
            pltpu.VMEM((2, HALF // 2, WL), bf),
            dma((4,)),
            dma((6,)), dma((6,)),
            dma((NF,)), dma((NF,)),
            dma((2, NF)), dma((2, NF)),
            dma((NF,)), dma,
            dma((NZ,)), dma((NZ,)), dma((NZ,)),
            dma((NX,)), dma((NX + 2,)),
            dma((2, 6)), dma((2, 6)),
        ],
        compiler_params=pltpu.CompilerParams(
            collective_id=ident, has_side_effects=True, vmem_limit_bytes=56 * 1024 * 1024
        ),
    )(kinds, qkv, weight)


def local(qkv, head_kinds, out_weight):
    chip = jnp.arange(NY * HC) // HC == jnp.arange(NY)[:, None]
    counts = jnp.sum(jnp.where(chip, head_kinds, 0), axis=1)
    more = jnp.maximum(counts - SIZES[0][0], 0)[:, None]
    fewer = jnp.maximum(HC - SIZES[0][1] - counts, 0)[None, :]
    index = jnp.max(jnp.where((more > 1) | (fewer > 1), len(SIZES) - 1, 2 * more + fewer))
    choices = [
        functools.partial(attention, slots, frees, ident)
        for ident, (slots, frees) in enumerate(SIZES)
    ]
    return lax.switch(index, choices, head_kinds, qkv.transpose(1, 0, 2), out_weight)


def solution(mesh):
    placed = (P("frame", None, "head"), P(), P("head", None))
    return jax.shard_map(
        local, mesh=mesh, in_specs=placed, out_specs=P("frame", "head"), check_vma=False
    )
```
